256 devices in a mesh: img: 8 (over z_hi, x), txt: 32 (over z_lo, y, core).
Axes of the slice: x: 4, y: 4, z: 8 (z_hi: 2, z_lo: 4; z = z_hi * 4 + z_lo), core: 2. Of those that a mesh axis runs over, the one named last changes fastest.
Arguments:
- image_emb: bfloat16 [20480, 1152], P(('img', 'txt'))
- text_emb: bfloat16 [20480, 1152], P(('txt', 'img'))
- partner: int32 [20480], P('img'), may hold values from 0 to 20479, as said below
- log_scale: float32 [1], replicated, may hold values from 2 to 3
- bias: float32 [1], replicated, may hold values from -6 to -2
Outputs:
- loss: float32 [1], replicated
- grad_image: float32 [20480, 1152], P(('img', 'txt'))
- grad_text: float32 [20480, 1152], P(('txt', 'img'))
The draws below stay inside these ranges and needn't reach their ends.
Inputs may be any that keep to these rules, and one draw needn't show every extreme that they name: partner is a permutation: each text row is paired with exactly one image row.
All inputs are finite; a program needn't handle non-finite values.
Results may differ from the reference program's by a relative error of at most 0.00099.
Values may be sent and summed in bfloat16 or wider, within the bound.
A program may use at most 64 MiB of HBM per device.

```python
import math
import jax
import jax.numpy as jnp
from jax import lax

D = 1152
PAIRS = 20480


def shared_parts(key):
    pairing = jax.random.permutation(jax.random.fold_in(key, 11), PAIRS).astype(jnp.int32)
    centers = jax.random.normal(jax.random.fold_in(key, 12), (8, D), jnp.float32)
    weights = jax.random.normal(jax.random.fold_in(key, 13), (PAIRS, 8), jnp.float32) * (1.0 / math.sqrt(8.0))
    latent = jax.random.normal(jax.random.fold_in(key, 14), (PAIRS, D), jnp.float32)
    spread = jax.random.uniform(jax.random.fold_in(key, 15), (D,), jnp.float32, math.log(0.35), math.log(3.5))
    cluster = weights[:, 0:1] * centers[0][None, :]
    for member in range(1, 8):
        cluster = cluster + weights[:, member:member + 1] * centers[member][None, :]
    return (pairing, cluster, latent, jnp.exp(spread))


def compose(cluster, latent, noise, row_scale, columns):
    mixed = 0.59 * cluster + 0.45 * latent + 0.67 * noise
    return row_scale * columns[None, :] * mixed


def draw_partner(key, part):
    pairing, cluster, latent, columns = shared_parts(key)
    return pairing


def draw_image_emb(key, part):
    pairing, cluster, latent, columns = shared_parts(key)
    key = jax.random.fold_in(key, 1)
    noise = jax.random.normal(jax.random.fold_in(key, 2), (PAIRS, D), jnp.float32)
    row_log = jax.random.uniform(jax.random.fold_in(key, 3), (PAIRS, 1), jnp.float32, math.log(0.3), math.log(3.0))
    values = compose(cluster, latent, noise, jnp.exp(row_log), columns)
    return values.astype(jnp.bfloat16)


def draw_text_emb(key, part):
    pairing, cluster, latent, columns = shared_parts(key)
    key = jax.random.fold_in(key, 2)
    cluster_text = jnp.zeros((PAIRS, D), jnp.float32).at[pairing].set(cluster)
    latent_text = jnp.zeros((PAIRS, D), jnp.float32).at[pairing].set(latent)
    noise = jax.random.normal(jax.random.fold_in(key, 4), (PAIRS, D), jnp.float32)
    row_log = jax.random.uniform(jax.random.fold_in(key, 5), (PAIRS, 1), jnp.float32, math.log(0.3), math.log(3.0))
    values = compose(cluster_text, latent_text, noise, jnp.exp(row_log), columns)
    return values.astype(jnp.bfloat16)


def setup_inputs(seed: int = 0) -> dict:
    seeds = jax.random.split(jax.random.key(seed), 6)
    return {
        "image_emb": draw_image_emb(jax.random.fold_in(seeds[5], 71), 0),
        "text_emb": draw_text_emb(jax.random.fold_in(seeds[5], 71), 0),
        "partner": draw_partner(jax.random.fold_in(seeds[5], 71), 0),
        "log_scale": jnp.clip(jax.random.uniform(seeds[3], (1,), jnp.float32, 2.0, 3.0), 2.0, 3.0),
        "bias": jnp.clip(jax.random.uniform(seeds[4], (1,), jnp.float32, -6.0, -2.0), -6.0, -2.0),
    }


def normalize(emb):
    full = emb.astype(jnp.float32)
    inverse = lax.rsqrt(lax.optimization_barrier(jnp.sum(full * full, axis=1, keepdims=True)) + 1e-06)
    return (full * inverse, inverse)

def back_norm(unit, inverse, direction):
    inner = lax.optimization_barrier(jnp.sum(unit * direction, axis=1, keepdims=True))
    return inverse * (direction - unit * inner)

def reference(image_emb, text_emb, partner, log_scale, bias):
    image_unit, image_inv = normalize(image_emb)
    text_unit, text_inv = normalize(text_emb)
    image_wire = image_unit.astype(jnp.bfloat16)
    text_wire = text_unit.astype(jnp.bfloat16)
    scale = jnp.exp(log_scale[0])
    shift = bias[0]
    block = math.gcd(PAIRS, 512)
    columns = lax.iota(jnp.int32, PAIRS)

    def step(carry, index):
        text_acc, loss_acc = carry
        start = (index * block).astype(jnp.int32)
        piece = lax.dynamic_slice_in_dim(image_wire, start, block, 0)
        mates = lax.dynamic_slice_in_dim(partner, start, block, 0)
        cosine = jnp.dot(piece, text_wire.T, preferred_element_type=jnp.float32)
        logits = scale * cosine + shift
        positive = (mates[:, None] == columns[None, :]).astype(jnp.float32)
        signed = 2.0 * positive - 1.0
        part_loss = jnp.sum(jax.nn.softplus(-signed * logits))
        slope = (jax.nn.sigmoid(logits) - positive).astype(jnp.bfloat16)
        image_part = jnp.dot(slope, text_wire, preferred_element_type=jnp.float32)
        text_acc = text_acc + jnp.dot(slope.T, piece, preferred_element_type=jnp.float32)
        return ((text_acc, loss_acc + part_loss), image_part)
    start_carry = (jnp.zeros((PAIRS, D), jnp.float32), jnp.zeros((), jnp.float32))
    (text_acc, loss_acc), image_parts = lax.scan(step, start_carry, jnp.arange(PAIRS // block, dtype=jnp.int32))
    image_dir = scale * image_parts.reshape(PAIRS, D)
    text_dir = scale * text_acc
    loss = (loss_acc / PAIRS).reshape(1)
    grad_image = back_norm(image_unit, image_inv, image_dir)
    grad_text = back_norm(text_unit, text_inv, text_dir)
    return (loss, grad_image, grad_text)
```

```python
import functools
import math

import jax
import jax.numpy as jnp
from jax import lax
from jax.experimental import pallas as pl
from jax.experimental.pallas import tpu as pltpu
from jax.sharding import PartitionSpec as P

MESH = pl.DeviceIdType.MESH
F32, BF16 = jnp.float32, jnp.bfloat16
ROWS, D = 80, 1152
PAIRS = 20480
SIDE = 16 * ROWS
BUNDLE = 4 * ROWS
HALF = 8 * ROWS
CUT = 48
SENDS, RECVS = 96, 96


def normalize(emb):
    full = emb.astype(F32)
    inverse = lax.rsqrt(jnp.sum(full * full, axis=1, keepdims=True) + 1e-06)
    return (full * inverse, inverse)


def back_norm(unit, inverse, direction):
    inner = jnp.sum(unit * direction, axis=1, keepdims=True)
    return inverse * (direction - unit * inner)


def at(slot, first=0, count=ROWS):
    return pl.ds(pl.multiple_of(slot * ROWS + first, 16), count)


class Links:
    def __init__(self, send, recv):
        self.send, self.recv = send, recv
        self.sent = []
        self.used = 0

    def ticket(self):
        self.used += 1
        return self.used - 1

    def start(self, src, dst, ticket, device):
        copy = pltpu.make_async_remote_copy(
            src_ref=src,
            dst_ref=dst,
            send_sem=self.send.at[len(self.sent)],
            recv_sem=self.recv.at[ticket],
            device_id=device,
            device_id_type=MESH,
        )
        copy.start()
        self.sent.append(copy)

    def arrived(self, dst, ticket):
        pltpu.make_async_copy(dst, dst, self.recv.at[ticket]).wait()

    def drain(self):
        for copy in self.sent:
            copy.wait_send()


def kernel(
    image_ref, text_ref, table_ref, log_scale_ref, bias_ref,
    loss_ref, grad_image_ref, grad_text_ref,
    imgs, txts, slopes, pimg, ptxt,
    mates, mate_rows, mate_cols, text_ids, loss_acc,
    b_far, b_near, a_far, a_near, sib, z_in,
    loss_x, loss_y, loss_z, loss_c,
    send_sems, recv_sems,
):
    img, txt = lax.axis_index("img"), lax.axis_index("txt")
    x, z_hi = img % 4, img // 4
    core, y, z_lo = txt % 2, (txt // 2) % 4, txt // 8
    z = z_hi * 4 + z_lo

    def dev(x, y, z, core):
        return {"img": (z // 4) * 4 + x, "txt": ((z % 4) * 4 + y) * 2 + core}

    def swap(a, b):
        return a + core * (b - a), b + core * (a - b)

    a, b = swap(x, y)

    def plane(a, b):
        px, py = swap(a % 4, b % 4)
        return dev(px, py, z, core)

    def along_z(k):
        return dev(x, y, (z + k) % 8, core)

    a_next, a_prev = plane(a + 1, b), plane(a + 3, b)
    b_next, b_prev = plane(a, b + 1), plane(a, b + 3)
    z_next, z_prev = along_z(1), along_z(7)
    sibling = dev(x, y, z, 1 - core)
    links = Links(send_sems, recv_sems)

    barrier = pltpu.get_barrier_semaphore()
    partners = [dev((x + k) % 4, y, z, core) for k in (1, 2, 3)]
    partners += [dev(x, (y + k) % 4, z, core) for k in (1, 2, 3)]
    partners += [along_z(k) for k in range(1, 8)] + [sibling]
    for device in partners:
        pl.semaphore_signal(barrier, inc=1, device_id=device, device_id_type=MESH)

    def img_slot(a, b):
        return (b % 4) * 4 + a % 4

    own = img_slot(a, b)
    own_text = core * 8 + z
    imgs[at(own), :] = normalize(image_ref[...])[0].astype(BF16)
    txts[at(own_text), :] = normalize(text_ref[...])[0].astype(BF16)
    mates[x] = table_ref[pl.ds(pl.multiple_of(z_lo * 8, 8), 8), :]
    pl.semaphore_wait(barrier, len(partners))

    def send_img(slot, ticket, device, first=0, count=ROWS):
        view = imgs.at[at(slot, first, count), :]
        links.start(view, view, ticket, device)

    def got_img(slot, ticket, first=0, count=ROWS):
        links.arrived(imgs.at[at(slot, first, count), :], ticket)

    def send_txt(slot, ticket, device, first=0, count=ROWS):
        view = txts.at[at(slot, first, count), :]
        links.start(view, view, ticket, device)

    def got_txt(slot, ticket, first=0, count=ROWS):
        links.arrived(txts.at[at(slot, first, count), :], ticket)

    ta = [links.ticket() for _ in range(4)]
    tb_next = [links.ticket() for _ in range(4)]
    tb_prev = [links.ticket() for _ in range(4)]
    tb_far = [links.ticket() for _ in range(4)]
    tz_next = [links.ticket() for _ in range(4)]
    tz_prev = [links.ticket() for _ in range(4)]
    t_sib = [links.ticket() for _ in range(8)]
    t_mates = [links.ticket() for _ in range(3)]

    order = [0, 3, 1, 2]

    def send_b(k):
        slot = img_slot(a + order[k], b)
        send_img(slot, tb_next[k], b_next)
        send_img(slot, tb_prev[k], b_prev)

    def forward_b(k):
        got_img(img_slot(a + order[k], b + 3), tb_next[k])
        got_img(img_slot(a + order[k], b + 1), tb_prev[k])
        if k % 2 == 0:
            send_img(img_slot(a + order[k], b + 3), tb_far[k], b_next)
        else:
            send_img(img_slot(a + order[k], b + 1), tb_far[k], b_prev)

    def z_slot(k):
        return core * 8 + (z + k) % 8

    def send_sib(k):
        send_txt(z_slot(k), t_sib[k], sibling)

    send_img(own, ta[0], a_next)
    send_img(own, ta[1], a_prev)
    send_txt(own_text, tz_next[0], z_next)
    send_txt(own_text, tz_prev[0], z_prev)
    send_b(0)
    for k in (1, 2, 3):
        links.start(mates.at[x], mates.at[x], t_mates[k - 1], partners[k - 1])
    send_sib(0)

    got_img(img_slot(a + 3, b), ta[0])
    send_img(img_slot(a + 3, b), ta[2], a_next, 0, CUT)
    got_img(img_slot(a + 1, b), ta[1])
    send_img(img_slot(a + 1, b), ta[3], a_prev, CUT, ROWS - CUT)
    for h in (1, 2, 3):
        last = h == 3
        got_txt(z_slot(-h), tz_next[h - 1])
        send_txt(z_slot(-h), tz_next[h], z_next, 0, CUT if last else ROWS)
        got_txt(z_slot(h), tz_prev[h - 1])
        if last:
            send_txt(z_slot(h), tz_prev[h], z_prev, CUT, ROWS - CUT)
        else:
            send_txt(z_slot(h), tz_prev[h], z_prev)
        send_sib(8 - h)
        send_sib(h)
        if h == 1:
            send_b(1)
            send_b(2)
            forward_b(0)
        if h == 2:
            got_img(img_slot(a + 2, b), ta[2], 0, CUT)
            got_img(img_slot(a + 2, b), ta[3], CUT, ROWS - CUT)
            send_b(3)
            forward_b(1)
            forward_b(2)
    got_txt(z_slot(4), tz_next[3], 0, CUT)
    got_txt(z_slot(4), tz_prev[3], CUT, ROWS - CUT)
    send_sib(4)
    forward_b(3)

    for k in (1, 2, 3):
        links.arrived(mates.at[(x + 4 - k) % 4], t_mates[k - 1])
    mate_rows[...] = jnp.zeros_like(mate_rows)
    for slot in range(16):
        px, py = swap(slot % 4, slot // 4)
        mate_rows[slot:slot + 1, :] = mates[px, pl.ds(2 * py + core, 1), :].astype(F32)
    turned = mate_rows[...].T
    for slot in range(16):
        mate_cols[slot * ROWS:(slot + 1) * ROWS, :] = jnp.broadcast_to(
            turned[0:ROWS, slot:slot + 1], (ROWS, 128)
        )
    column = lax.broadcasted_iota(jnp.int32, (8, SIDE), 1)
    ids = column
    for slot in range(16):
        c, pz = slot // 8, slot % 8
        start = ((((pz % 4) * 4 + y) * 2 + c) * 8 + (pz // 4) * 4 + x) * ROWS
        ids = jnp.where(column >= slot * ROWS, column - slot * ROWS + start, ids)
    text_ids[...] = ids.astype(F32)

    for k in range(8):
        got_txt((1 - core) * 8 + (z + k) % 8, t_sib[k])
    for k in range(4):
        got_img(img_slot(a + order[k], b + 2), tb_far[k])

    scale = jnp.exp(jnp.full((1, 1), log_scale_ref[0], F32))
    to_log2 = scale * math.log2(math.e)
    shift = jnp.full((1, 1), bias_ref[0] * math.log2(math.e), F32)
    loss_acc[...] = jnp.zeros_like(loss_acc)

    def tile(step, _):
        rows = pl.ds(pl.multiple_of((step // 5) * BUNDLE, BUNDLE), BUNDLE)
        cols = pl.ds(pl.multiple_of((step % 5) * 256, 256), 256)
        cosine = lax.dot_general(
            imgs[rows, :], txts[cols, :], (((1,), (1,)), ((), ())), preferred_element_type=F32
        )
        logits = cosine * to_log2 + shift
        e = jnp.exp2(logits)
        u = 1.0 + e
        r = 1.0 / u
        mate = mate_cols[rows, :]
        positive = jnp.concatenate([mate, mate], axis=1) == text_ids[0:1, cols]
        slopes[rows, cols] = jnp.where(positive, -r, e * r).astype(BF16)
        small = e < 0.015625
        series = e * (1.0 - e * (0.5 - e * (1.0 / 3.0 - e * 0.25)))
        factor = jnp.where(small, 1.0, u)
        term = jnp.where(small, series, 0.0) - jnp.where(positive, logits * math.log(2.0), 0.0)
        product = factor[0:80] * factor[80:160] * factor[160:240] * factor[240:320]
        total = jnp.log(product).reshape(10, 8, 256).sum(0) + term.reshape(40, 8, 256).sum(0)
        loss_acc[...] += total
        return 0

    lax.fori_loop(0, 20, tile, 0)

    lx = [links.ticket() for _ in range(3)]
    ly = [links.ticket() for _ in range(3)]
    lz = [links.ticket() for _ in range(7)]
    lc = links.ticket()

    def share(buffer, me, size, tickets, devices):
        for k in range(1, size):
            links.start(buffer.at[me], buffer.at[me], tickets[k - 1], devices[k - 1])

    def gathered(buffer, me, size, tickets):
        for k in range(1, size):
            links.arrived(buffer.at[(me + size - k) % size], tickets[k - 1])
        total = buffer[0]
        for k in range(1, size):
            total = total + buffer[k]
        return total

    part = jnp.sum(jnp.sum(loss_acc[...], axis=0, keepdims=True), axis=1, keepdims=True)
    loss_x[x] = jnp.broadcast_to(part, (8, 128))
    share(loss_x, x, 4, lx, partners[0:3])

    def image_part(bundle):
        rows = pl.ds(pl.multiple_of((bundle % 4) * BUNDLE, BUNDLE), BUNDLE)

        def chunk(n, _):
            cols = pl.ds(pl.multiple_of(n * 384, 384), 384)
            pimg[rows, cols] = jnp.dot(slopes[rows, :], txts[:, cols], preferred_element_type=F32)
            return 0

        lax.fori_loop(0, 3, chunk, 0)

    def text_part(half):
        rows = pl.ds(pl.multiple_of(half * HALF, 128), HALF)

        def chunk(n, _):
            cols = pl.ds(pl.multiple_of(n * 384, 384), 384)
            ptxt[rows, cols] = lax.dot_general(
                slopes[:, rows], imgs[:, cols], (((0,), (0,)), ((), ())), preferred_element_type=F32
            )
            return 0

        lax.fori_loop(0, 3, chunk, 0)

    def add(total, start, source, first, count):
        for k in range(0, count, 16):
            total[pl.ds(pl.multiple_of(start + k, 16), 16), :] += source[first + k:first + k + 16, :]

    ub_far = [links.ticket() for _ in range(2)]
    ub_near = [links.ticket() for _ in range(2)]
    ua_far = [links.ticket() for _ in range(2)]
    ua_near = [links.ticket() for _ in range(2)]
    uz = [[links.ticket() for _ in range(4)] for _ in range(2)]
    u_sib = links.ticket()

    def bundle_at(k, first=0, count=BUNDLE):
        return pl.ds(pl.multiple_of(((b + k) % 4) * BUNDLE + first, 16), count)

    image_part(b + 2)
    links.start(pimg.at[bundle_at(2, 0, 160), :], b_far.at[0], ub_far[0], b_next)
    links.start(pimg.at[bundle_at(2, 160, 160), :], b_far.at[1], ub_far[1], b_prev)
    text_part(1 - core)
    links.start(ptxt.at[pl.ds(pl.multiple_of((1 - core) * HALF, 16), HALF), :], sib, u_sib, sibling)
    loss_y[y] = gathered(loss_x, x, 4, lx)
    share(loss_y, y, 4, ly, partners[3:6])
    image_part(b + 1)
    links.arrived(b_far.at[0], ub_far[0])
    add(pimg, ((b + 1) % 4) * BUNDLE, b_far.at[0], 0, 160)
    links.start(pimg.at[bundle_at(1), :], b_near.at[0], ub_near[0], b_next)
    image_part(b + 3)
    links.arrived(b_far.at[1], ub_far[1])
    add(pimg, ((b + 3) % 4) * BUNDLE + 160, b_far.at[1], 0, 160)
    links.start(pimg.at[bundle_at(3), :], b_near.at[1], ub_near[1], b_prev)
    text_part(core)
    links.arrived(sib, u_sib)
    add(ptxt, core * HALF, sib, 0, HALF)

    def z_at(k, first=0, count=ROWS):
        return ptxt.at[at(core * 8 + (z + k) % 8, first, count), :]

    def z_start(k):
        return (core * 8 + (z + k) % 8) * ROWS

    rest = ROWS - CUT
    links.start(z_at(4, 0, CUT), z_in.at[0, 3, pl.ds(0, CUT), :], uz[0][3], z_next)
    links.start(z_at(4, CUT, rest), z_in.at[1, 3, pl.ds(0, rest), :], uz[1][3], z_prev)
    loss_z[z] = gathered(loss_y, y, 4, ly)
    share(loss_z, z, 8, lz, partners[6:13])
    image_part(b)

    links.arrived(z_in.at[0, 3, pl.ds(0, CUT), :], uz[0][3])
    add(ptxt, z_start(3), z_in.at[0, 3], 0, CUT)
    links.start(z_at(3), z_in.at[0, 2], uz[0][2], z_next)
    links.arrived(z_in.at[1, 3, pl.ds(0, rest), :], uz[1][3])
    add(ptxt, z_start(5) + CUT, z_in.at[1, 3], 0, rest)
    links.start(z_at(5), z_in.at[1, 2], uz[1][2], z_prev)

    def a_start(k):
        return img_slot(a + k, b) * ROWS

    links.arrived(b_near.at[0], ub_near[0])
    links.arrived(b_near.at[1], ub_near[1])

    def fold(k):
        start = a_start(k)
        offset = ((a + k) % 4) * ROWS
        for n in range(0, ROWS, 16):
            here = pl.ds(pl.multiple_of(start + n, 16), 16)
            there = pl.ds(pl.multiple_of(offset + n, 16), 16)
            pimg[here, :] += b_near[0, there, :] + b_near[1, there, :]

    fold(2)
    links.start(pimg.at[at(img_slot(a + 2, b), 0, CUT), :], a_far.at[0], ua_far[0], a_next)
    links.start(pimg.at[at(img_slot(a + 2, b), CUT, rest), :], a_far.at[1, pl.ds(0, rest), :], ua_far[1], a_prev)
    fold(1)
    fold(3)
    fold(0)

    for h in (2, 1):
        links.arrived(z_in.at[0, h], uz[0][h])
        add(ptxt, z_start(h), z_in.at[0, h], 0, ROWS)
        links.start(z_at(h), z_in.at[0, h - 1], uz[0][h - 1], z_next)
        links.arrived(z_in.at[1, h], uz[1][h])
        add(ptxt, z_start(8 - h), z_in.at[1, h], 0, ROWS)
        links.start(z_at(8 - h), z_in.at[1, h - 1], uz[1][h - 1], z_prev)
        if h == 2:
            links.arrived(a_far.at[0], ua_far[0])
            add(pimg, a_start(1), a_far.at[0], 0, CUT)
            links.start(pimg.at[at(img_slot(a + 1, b)), :], a_near.at[0], ua_near[0], a_next)
            links.arrived(a_far.at[1, pl.ds(0, rest), :], ua_far[1])
            add(pimg, a_start(3) + CUT, a_far.at[1], 0, rest)
            links.start(pimg.at[at(img_slot(a + 3, b)), :], a_near.at[1], ua_near[1], a_prev)

    loss_c[core] = gathered(loss_z, z, 8, lz)
    share(loss_c, core, 2, [lc], [sibling])
    links.arrived(a_near.at[0], ua_near[0])
    links.arrived(a_near.at[1], ua_near[1])
    image_sum = pimg[at(own), :] + a_near[0] + a_near[1]
    unit, inverse = normalize(image_ref[...])
    grad_image_ref[...] = back_norm(unit, inverse, scale * image_sum)

    links.arrived(z_in.at[0, 0], uz[0][0])
    links.arrived(z_in.at[1, 0], uz[1][0])
    text_sum = ptxt[at(own_text), :] + z_in[0, 0] + z_in[1, 0]
    unit, inverse = normalize(text_ref[...])
    grad_text_ref[...] = back_norm(unit, inverse, scale * text_sum)
    loss_ref[...] = gathered(loss_c, core, 2, [lc]) * (1.0 / PAIRS)
    links.drain()


def on_device(image_emb, text_emb, partner, log_scale, bias):
    table = jnp.pad(partner.reshape(32, ROWS), ((0, 0), (0, 128 - ROWS)))
    vmem, smem = pl.BlockSpec(memory_space=pltpu.VMEM), pl.BlockSpec(memory_space=pltpu.SMEM)
    loss, grad_image, grad_text = pl.pallas_call(
        kernel,
        out_shape=(
            jax.ShapeDtypeStruct((8, 128), F32),
            jax.ShapeDtypeStruct((ROWS, D), F32),
            jax.ShapeDtypeStruct((ROWS, D), F32),
        ),
        in_specs=[vmem, vmem, vmem, smem, smem],
        out_specs=(vmem, vmem, vmem),
        scratch_shapes=[
            pltpu.VMEM((SIDE, D), BF16),
            pltpu.VMEM((SIDE, D), BF16),
            pltpu.VMEM((SIDE, SIDE), BF16),
            pltpu.VMEM((SIDE, D), F32),
            pltpu.VMEM((SIDE, D), F32),
            pltpu.VMEM((4, 8, 128), jnp.int32),
            pltpu.VMEM((128, 128), F32),
            pltpu.VMEM((SIDE, 128), F32),
            pltpu.VMEM((8, SIDE), F32),
            pltpu.VMEM((8, 256), F32),
            pltpu.VMEM((2, 160, D), F32),
            pltpu.VMEM((2, BUNDLE, D), F32),
            pltpu.VMEM((2, CUT, D), F32),
            pltpu.VMEM((2, ROWS, D), F32),
            pltpu.VMEM((HALF, D), F32),
            pltpu.VMEM((2, 4, ROWS, D), F32),
            pltpu.VMEM((4, 8, 128), F32),
            pltpu.VMEM((4, 8, 128), F32),
            pltpu.VMEM((8, 8, 128), F32),
            pltpu.VMEM((2, 8, 128), F32),
            pltpu.SemaphoreType.DMA((SENDS,)),
            pltpu.SemaphoreType.DMA((RECVS,)),
        ],
        compiler_params=pltpu.CompilerParams(
            collective_id=0, has_side_effects=True, vmem_limit_bytes=60 * 1024 * 1024
        ),
    )(image_emb, text_emb, table, log_scale, bias)
    return (loss[0, 0:1], grad_image, grad_text)


def solution(mesh):
    return jax.shard_map(
        on_device,
        mesh=mesh,
        in_specs=(P(("img", "txt"), None), P(("txt", "img"), None), P("img"), P(), P()),
        out_specs=(P(), P(("img", "txt"), None), P(("txt", "img"), None)),
        check_vma=False,
    )
```

```python
import math

import jax
import jax.numpy as jnp
from jax import lax
from jax.experimental import pallas as pl
from jax.experimental.pallas import tpu as pltpu
from jax.sharding import PartitionSpec as P

MESH = pl.DeviceIdType.MESH
F32, BF16, I16 = jnp.float32, jnp.bfloat16, jnp.int16
ROWS, D = 80, 1152
PAIRS = 20480
SIDE = 16 * ROWS
BUNDLE = 4 * ROWS
OFF4 = (0, 1, 3, 2)
OFF8 = (0, 1, 7, 2, 6, 3, 5, 4)
KEY4 = {off: k for k, off in enumerate(OFF4)}
KEY8 = {off: k for k, off in enumerate(OFF8)}
PIECES = ((0, 32), (32, 16), (48, 32))
FULL = ((0, 1), (2,))
COUNT = 224


def normalize(emb):
    full = emb.astype(F32)
    inverse = lax.rsqrt(jnp.sum(full * full, axis=1, keepdims=True) + 1e-06)
    return (full * inverse, inverse)


def back_norm(unit, inverse, direction):
    inner = jnp.sum(unit * direction, axis=1, keepdims=True)
    return inverse * (direction - unit * inner)


class Links:
    def __init__(self, send, recv):
        self.send, self.recv = send, recv
        self.sent = []
        self.used = 0

    def tickets(self, count):
        self.used += count
        assert self.used <= COUNT
        return list(range(self.used - count, self.used))

    def start(self, src, dst, ticket, device):
        copy = pltpu.make_async_remote_copy(
            src_ref=src,
            dst_ref=dst,
            send_sem=self.send.at[len(self.sent)],
            recv_sem=self.recv.at[ticket],
            device_id=device,
            device_id_type=MESH,
        )
        copy.start()
        self.sent.append(copy)

    def arrived(self, dst, ticket):
        pltpu.make_async_copy(dst, dst, self.recv.at[ticket]).wait()

    def drain(self):
        for copy in self.sent:
            copy.wait_send()


def by_lanes(body):
    def step(n, _):
        for k in range(3):
            body(pl.ds(pl.multiple_of((n * 3 + k) * 128, 128), 128))
        return 0

    lax.fori_loop(0, D // 384, step, 0)


def widen(q, s, rows, lanes):
    return q[rows, lanes].astype(F32) * s[:, lanes]


def narrow(value, q, s, rows):
    def body(lanes):
        v = value(lanes)
        top = jnp.maximum(jnp.max(jnp.abs(v), axis=0, keepdims=True), 1e-30)
        q[rows, lanes] = jnp.round(v * (32767.0 * pltpu.reciprocal(top, approx=True))).astype(I16)
        s[:, lanes] = top * (1.0 / 32767.0)

    by_lanes(body)


def kernel(
    image_ref, text_ref, table_ref, log_scale_ref, bias_ref,
    loss_ref, grad_image_ref, grad_text_ref,
    imgs, txts, slopes, pimg, ptxt,
    mates, mate_rows, mate_all, mate_cols, text_ids, loss_acc,
    far_q, far_s, far_qi, far_si,
    near_q, near_s, near_qi, near_si,
    a_q, a_s, a_qi, a_si,
    sib_q, sib_s, sib_qi, sib_si,
    z_q, z_s, z_qi, z_si,
    loss_x, loss_y, loss_z, loss_c,
    send_sems, recv_sems,
):
    img, txt = lax.axis_index("img"), lax.axis_index("txt")
    x, z_hi = img % 4, img // 4
    core, y, z_lo = txt % 2, (txt // 2) % 4, txt // 8
    z = z_hi * 4 + z_lo

    def dev(x, y, z, core):
        return {"img": (z // 4) * 4 + x, "txt": ((z % 4) * 4 + y) * 2 + core}

    def swap(a, b):
        return a + core * (b - a), b + core * (a - b)

    a, b = swap(x, y)

    def plane(a, b):
        px, py = swap(a % 4, b % 4)
        return dev(px, py, z, core)

    def along_z(k):
        return dev(x, y, (z + k) % 8, core)

    to_a = [plane(a + off, b) for off in OFF4]
    to_b = (plane(a, b + 1), plane(a, b + 3))
    to_z = (along_z(1), along_z(7))
    sibling = dev(x, y, z, 1 - core)
    links = Links(send_sems, recv_sems)

    barrier = pltpu.get_barrier_semaphore()
    partners = [dev((x + k) % 4, y, z, core) for k in (1, 2, 3)]
    partners += [dev(x, (y + k) % 4, z, core) for k in (1, 2, 3)]
    partners += [along_z(k) for k in range(1, 8)] + [sibling]
    for device in partners:
        pl.semaphore_signal(barrier, inc=1, device_id=device, device_id_type=MESH)

    imgs[0:ROWS, :] = normalize(image_ref[...])[0].astype(BF16)
    txts[0:ROWS, :] = normalize(text_ref[...])[0].astype(BF16)
    for k in range(5):
        mates[x, k:k + 1, :] = table_ref[pl.ds(z_lo * 5 + k, 1), :]
    loss_acc[...] = jnp.zeros_like(loss_acc)
    pl.semaphore_wait(barrier, len(partners))

    def img_at(kb, ka):
        return imgs.at[pl.ds((kb * 4 + ka) * ROWS, ROWS), :]

    def txt_at(kz, cc, first=0, count=ROWS):
        return txts.at[pl.ds((kz * 2 + cc) * ROWS + first, count), :]

    ta = links.tickets(4)
    tb = [links.tickets(4) for _ in range(2)]
    tb_far = links.tickets(4)
    tz = [[links.tickets(3) for _ in range(4)] for _ in range(2)]
    t_sib = links.tickets(8)
    t_mates = links.tickets(3)

    def b_key(direction):
        return KEY4[3 if direction == 0 else 1]

    def z_key(direction, h):
        return KEY8[-h % 8 if direction == 0 else h]

    def send_b(ka):
        for d in (0, 1):
            links.start(img_at(0, ka), img_at(b_key(d), ka), tb[d][ka], to_b[d])

    def got_b(ka):
        for d in (0, 1):
            links.arrived(img_at(b_key(d), ka), tb[d][ka])
            if ka % 2 == d:
                links.start(img_at(b_key(d), ka), img_at(3, ka), tb_far[ka], to_b[d])

    def send_z(d, h, p):
        first, count = PIECES[p]
        links.start(
            txt_at(z_key(d, h - 1) if h > 1 else 0, 0, first, count),
            txt_at(z_key(d, h), 0, first, count),
            tz[d][h - 1][p],
            to_z[d],
        )

    def got_z(h):
        for p in (0, 2, 1):
            for d in (0, 1):
                if h == 4 and p not in FULL[d]:
                    continue
                first, count = PIECES[p]
                links.arrived(txt_at(z_key(d, h), 0, first, count), tz[d][h - 1][p])
                if h < 3 or (h == 3 and p in FULL[d]):
                    send_z(d, h + 1, p)

    def send_sib(kz):
        links.start(txt_at(kz, 0), txt_at(kz, 1), t_sib[kz], sibling)

    def got_sib(kz):
        links.arrived(txt_at(kz, 1), t_sib[kz])

    for p in (0, 2, 1):
        for d in (0, 1):
            send_z(d, 1, p)
    for ka in (3, 1, 2):
        off = OFF4[ka]
        links.start(img_at(0, 0), img_at(0, KEY4[-off % 4]), ta[ka], to_a[ka])
    send_b(0)
    send_sib(0)
    for k in (1, 2, 3):
        links.start(mates.at[x], mates.at[x], t_mates[k - 1], partners[k - 1])

    column = lax.broadcasted_iota(jnp.int32, (8, SIDE), 1)
    ids = column
    for kz in range(8):
        for cc in (0, 1):
            slot, pz = kz * 2 + cc, (z + OFF8[kz]) % 8
            c = core if cc == 0 else 1 - core
            start = ((((pz % 4) * 4 + y) * 2 + c) * 8 + (pz // 4) * 4 + x) * ROWS
            ids = jnp.where(column >= slot * ROWS, column - slot * ROWS + start, ids)
    text_ids[...] = ids.astype(F32)

    got_z(1)
    send_sib(1)
    send_sib(2)
    for ka in (1, 2, 3):
        links.arrived(img_at(0, KEY4[-OFF4[ka] % 4]), ta[ka])
        send_b(KEY4[-OFF4[ka] % 4])
    got_b(0)

    for k in (1, 2, 3):
        links.arrived(mates.at[(x + 4 - k) % 4], t_mates[k - 1])
    mate_rows[...] = jnp.zeros_like(mate_rows)
    for px in range(4):
        mate_rows[px * 8:px * 8 + 5, :] = mates[px, 0:5, :].astype(F32)
    turned = mate_rows[...].T
    for px in range(4):
        for k in range(5):
            mate_all[px, k * 128:(k + 1) * 128, :] = jnp.broadcast_to(
                turned[:, px * 8 + k:px * 8 + k + 1], (128, 128)
            )
    for kb in range(4):
        for ka in range(4):
            px, py = swap((a + OFF4[ka]) % 4, (b + OFF4[kb]) % 4)
            start = pl.multiple_of((2 * py + core) * ROWS, 16)
            mate_cols[(kb * 4 + ka) * ROWS:(kb * 4 + ka + 1) * ROWS, :] = mate_all[px, pl.ds(start, ROWS), :]

    scale = jnp.exp(jnp.full((1, 1), log_scale_ref[0], F32))
    to_log2 = scale * math.log2(math.e)
    shift = jnp.full((1, 1), bias_ref[0] * math.log2(math.e), F32)

    def tile(kb, first, count):
        rows = pl.ds(kb * BUNDLE if isinstance(kb, int) else pl.multiple_of(kb * BUNDLE, BUNDLE), BUNDLE)
        cols = pl.ds(first, count)
        cosine = lax.dot_general(
            imgs[rows, :], txts[cols, :], (((1,), (1,)), ((), ())), preferred_element_type=F32
        )
        logits = cosine * to_log2 + shift
        e = jnp.exp2(logits)
        u = 1.0 + e
        r = pltpu.reciprocal(u, approx=True)
        mate = mate_cols[rows, :]
        positive = jnp.concatenate([mate] * (count // 128), axis=1) == text_ids[0:1, cols]
        slopes[rows, cols] = jnp.where(positive, -r, e * r).astype(BF16)
        lost = (e - (u - 1.0)) * r
        paired = jnp.where(positive, logits, 0.0)
        product = u[0:80] * u[80:160] * u[160:240] * u[240:320]
        total = jnp.log(product).reshape(10, 8, count).sum(0)
        total += lost.reshape(40, 8, count).sum(0) - paired.reshape(40, 8, count).sum(0) * math.log(2.0)
        folded = total[:, 0:128]
        for k in range(128, count, 128):
            folded = folded + total[:, k:k + 128]
        loss_acc[...] += folded

    def tiles(low, high, first, count):
        def step(kb, _):
            tile(kb, first, count)
            return 0

        lax.fori_loop(low, high, step, 0)

    got_sib(0)
    got_sib(1)
    tile(0, 0, 256)
    got_z(2)
    send_sib(3)
    send_sib(4)
    got_b(1)
    got_b(2)
    got_sib(2)
    got_sib(3)
    got_sib(4)
    tile(0, 256, 512)
    got_z(3)
    send_sib(5)
    send_sib(6)
    got_b(3)
    tiles(1, 3, 0, 768)
    got_z(4)
    send_sib(7)
    got_sib(5)
    got_sib(6)
    got_sib(7)
    tiles(0, 3, 768, 512)
    for ka in range(4):
        links.arrived(img_at(3, ka), tb_far[ka])
    tile(3, 0, 1280)

    lx, ly, lz, lc = links.tickets(3), links.tickets(3), links.tickets(7), links.tickets(1)

    def share(buffer, me, size, tickets, devices):
        for k in range(1, size):
            links.start(buffer.at[me], buffer.at[me], tickets[k - 1], devices[k - 1])

    def gathered(buffer, me, size, tickets):
        for k in range(1, size):
            links.arrived(buffer.at[(me + size - k) % size], tickets[k - 1])
        total = buffer[0]
        for k in range(1, size):
            total = total + buffer[k]
        return total

    def image_part(kb):
        rows = pl.ds(kb * BUNDLE, BUNDLE)
        pimg[rows, :] = jnp.dot(slopes[rows, :], txts[...], preferred_element_type=F32)

    def text_part(first, count):
        rows = pl.ds(first, count)
        ptxt[rows, :] = lax.dot_general(
            slopes[:, rows], imgs[...], (((0,), (0,)), ((), ())), preferred_element_type=F32
        )

    whole = pl.ds(0, ROWS)

    def send_pair(q, s, q_in, s_in, tickets, device):
        links.start(q, q_in, tickets[0], device)
        links.start(s, s_in, tickets[1], device)

    def got_pair(q_in, s_in, tickets):
        links.arrived(q_in, tickets[0])
        links.arrived(s_in, tickets[1])

    def img_rows(kb, ka):
        return pl.ds((kb * 4 + ka) * ROWS, ROWS)

    FAR = ((3, 2), (1, 0))
    u_far = {ka: links.tickets(2) for ka in range(4)}
    u_near = [{ka: links.tickets(2) for ka in range(4)} for _ in range(2)]
    u_a = {ka: links.tickets(2) for ka in (1, 2, 3)}
    u_sib = [links.tickets(2) for _ in range(8)]
    u_z = [[[links.tickets(2) for _ in range(3)] for _ in range(4)] for _ in range(2)]

    def send_far():
        for n in (0, 1):
            for d in (0, 1):
                ka = FAR[d][n]
                narrow(lambda lanes: pimg[img_rows(3, ka), lanes], far_q.at[ka], far_s.at[ka], whole)
                send_pair(far_q.at[ka], far_s.at[ka], far_qi.at[ka], far_si.at[ka], u_far[ka], to_b[d])

    def send_near(d, ka):
        kb = KEY4[1 if d == 0 else 3]
        added = ka in FAR[d]
        if added:
            got_pair(far_qi.at[ka], far_si.at[ka], u_far[ka])

        def value(lanes):
            v = pimg[img_rows(kb, ka), lanes]
            return v + widen(far_qi.at[ka], far_si.at[ka], whole, lanes) if added else v

        n = d * 4 + ka
        narrow(value, near_q.at[n], near_s.at[n], whole)
        send_pair(near_q.at[n], near_s.at[n], near_qi.at[n], near_si.at[n], u_near[d][ka], to_b[d])

    def fold(ka):
        for d in (0, 1):
            got_pair(near_qi.at[d * 4 + ka], near_si.at[d * 4 + ka], u_near[d][ka])

        def value(lanes):
            v = pimg[img_rows(0, ka), lanes]
            return v + widen(near_qi.at[ka], near_si.at[ka], whole, lanes) + widen(
                near_qi.at[4 + ka], near_si.at[4 + ka], whole, lanes
            )

        if ka:
            narrow(value, a_q.at[ka], a_s.at[ka], whole)
            send_pair(a_q.at[ka], a_s.at[ka], a_qi.at[ka], a_si.at[ka], u_a[ka], to_a[ka])
        else:
            def body(lanes):
                pimg[0:ROWS, lanes] = value(lanes)

            by_lanes(body)

    def swap_text(kz):
        rows = pl.ds((kz * 2 + 1) * ROWS, ROWS)
        narrow(lambda lanes: ptxt[rows, lanes], sib_q.at[kz], sib_s.at[kz], whole)
        send_pair(sib_q.at[kz], sib_s.at[kz], sib_qi.at[kz], sib_si.at[kz], u_sib[kz], sibling)

    def got_swap(kz):
        got_pair(sib_qi.at[kz], sib_si.at[kz], u_sib[kz])

    def z_piece(buffer, d, r, p):
        return buffer.at[d * 4 + r - 1, pl.ds(*PIECES[p]), :]

    def z_step(d, r, p):
        return (d * 4 + r - 1) * 3 + p

    def got_zsum(d, r, p):
        got_pair(z_piece(z_qi, d, r, p), z_si.at[z_step(d, r, p)], u_z[d][r - 1][p])

    def send_zsum(d, r, p):
        first, count = PIECES[p]
        kz = KEY8[r % 8 if d == 0 else -r % 8]
        added = r < 3 or (r == 3 and p in FULL[d])
        if added:
            got_zsum(d, r + 1, p)
        here = pl.ds(first, count)

        def value(lanes):
            v = ptxt[pl.ds(kz * 2 * ROWS + first, count), lanes] + widen(sib_qi.at[kz], sib_si.at[kz], here, lanes)
            if added:
                v = v + widen(z_qi.at[d * 4 + r], z_si.at[z_step(d, r + 1, p)], here, lanes)
            return v

        n = z_step(d, r, p)
        narrow(value, z_q.at[d * 4 + r - 1], z_s.at[n], here)
        send_pair(
            z_piece(z_q, d, r, p), z_s.at[n], z_piece(z_qi, d, r, p), z_si.at[n], u_z[d][r - 1][p], to_z[d]
        )

    image_part(3)
    send_far()
    part = jnp.sum(jnp.sum(loss_acc[...], axis=0, keepdims=True), axis=1, keepdims=True)
    loss_x[x] = jnp.broadcast_to(part, (8, 128))
    share(loss_x, x, 4, lx, partners[0:3])
    text_part(768, 512)
    for kz in (7, 5, 6):
        swap_text(kz)
    image_part(1)
    image_part(2)
    send_near(0, 1)
    send_near(1, 3)
    got_swap(7)
    for p, d in ((0, 0), (2, 1), (1, 0)):
        send_zsum(d, 4, p)
    got_swap(5)
    got_swap(6)
    for p, d in ((2, 0), (0, 1), (1, 1)):
        send_zsum(d, 3, p)
    send_near(0, 3)
    send_near(1, 1)
    send_near(0, 0)
    send_near(1, 2)
    text_part(256, 512)
    for kz in (3, 4, 2):
        swap_text(kz)
    loss_y[y] = gathered(loss_x, x, 4, lx)
    share(loss_y, y, 4, ly, partners[3:6])
    send_near(0, 2)
    send_near(1, 0)
    for p, d in ((0, 0), (2, 1), (1, 0)):
        send_zsum(d, 3, p)
    text_part(0, 256)
    for kz in (1, 0):
        swap_text(kz)
    image_part(0)
    loss_z[z] = gathered(loss_y, y, 4, ly)
    share(loss_z, z, 8, lz, partners[6:13])
    got_swap(3)
    got_swap(4)
    for p, d in ((2, 0), (0, 1), (1, 1), (0, 0), (2, 1), (1, 0)):
        send_zsum(d, 2, p)
    fold(3)
    fold(1)
    got_swap(1)
    got_swap(2)
    for p, d in ((2, 0), (0, 1), (1, 1), (0, 0), (2, 1), (1, 0)):
        send_zsum(d, 1, p)
    fold(2)
    fold(0)
    loss_c[core] = gathered(loss_z, z, 8, lz)
    share(loss_c, core, 2, lc, [sibling])
    got_swap(0)

    for ka in (1, 2, 3):
        got_pair(a_qi.at[ka], a_si.at[ka], u_a[ka])

    def image_sum(lanes):
        v = pimg[0:ROWS, lanes]
        for ka in (1, 2, 3):
            v = v + widen(a_qi.at[ka], a_si.at[ka], whole, lanes)
        pimg[0:ROWS, lanes] = v

    by_lanes(image_sum)
    unit, inverse = normalize(image_ref[...])
    grad_image_ref[...] = back_norm(unit, inverse, scale * pimg[0:ROWS, :])

    for p, d in ((2, 0), (0, 1), (1, 1), (0, 0), (2, 1), (1, 0)):
        got_zsum(d, 1, p)

    def text_sum(lanes):
        for p, (first, count) in enumerate(PIECES):
            here = pl.ds(first, count)
            v = ptxt[here, lanes] + widen(sib_qi.at[0], sib_si.at[0], here, lanes)
            for d in (0, 1):
                v = v + widen(z_qi.at[d * 4], z_si.at[z_step(d, 1, p)], here, lanes)
            ptxt[here, lanes] = v

    by_lanes(text_sum)
    unit, inverse = normalize(text_ref[...])
    grad_text_ref[...] = back_norm(unit, inverse, scale * ptxt[0:ROWS, :])
    loss_ref[...] = gathered(loss_c, core, 2, lc) * (1.0 / PAIRS)
    links.drain()


def on_device(image_emb, text_emb, partner, log_scale, bias):
    vmem, smem = pl.BlockSpec(memory_space=pltpu.VMEM), pl.BlockSpec(memory_space=pltpu.SMEM)

    def messages(count):
        return [pltpu.VMEM((count, ROWS, D), I16), pltpu.VMEM((count, 1, D), F32)] * 2

    loss, grad_image, grad_text = pl.pallas_call(
        kernel,
        out_shape=(
            jax.ShapeDtypeStruct((8, 128), F32),
            jax.ShapeDtypeStruct((ROWS, D), F32),
            jax.ShapeDtypeStruct((ROWS, D), F32),
        ),
        in_specs=[vmem, vmem, vmem, smem, smem],
        out_specs=(vmem, vmem, vmem),
        scratch_shapes=[
            pltpu.VMEM((SIDE, D), BF16),
            pltpu.VMEM((SIDE, D), BF16),
            pltpu.VMEM((SIDE, SIDE), BF16),
            pltpu.VMEM((SIDE, D), F32),
            pltpu.VMEM((SIDE, D), F32),
            pltpu.VMEM((4, 8, 128), jnp.int32),
            pltpu.VMEM((128, 128), F32),
            pltpu.VMEM((4, 640, 128), F32),
            pltpu.VMEM((SIDE, 128), F32),
            pltpu.VMEM((8, SIDE), F32),
            pltpu.VMEM((8, 128), F32),
            *messages(4),
            *messages(8),
            *messages(4),
            *messages(8),
            *[pltpu.VMEM((8, ROWS, D), I16), pltpu.VMEM((24, 1, D), F32)] * 2,
            pltpu.VMEM((4, 8, 128), F32),
            pltpu.VMEM((4, 8, 128), F32),
            pltpu.VMEM((8, 8, 128), F32),
            pltpu.VMEM((2, 8, 128), F32),
            pltpu.SemaphoreType.DMA((COUNT,)),
            pltpu.SemaphoreType.DMA((COUNT,)),
        ],
        compiler_params=pltpu.CompilerParams(
            collective_id=0, has_side_effects=True, vmem_limit_bytes=60 * 1024 * 1024
        ),
    )(image_emb, text_emb, partner.reshape(20, 128), log_scale, bias)
    return (loss[0, 0:1], grad_image, grad_text)


def solution(mesh):
    return jax.shard_map(
        on_device,
        mesh=mesh,
        in_specs=(P(("img", "txt"), None), P(("txt", "img"), None), P("img"), P(), P()),
        out_specs=(P(), P(("img", "txt"), None), P(("txt", "img"), None)),
        check_vma=False,
    )
```

```python
import math

import jax
import jax.numpy as jnp
from jax import lax
from jax.experimental import pallas as pl
from jax.experimental.pallas import tpu as pltpu
from jax.sharding import PartitionSpec as P

MESH = pl.DeviceIdType.MESH
F32, BF16, I16 = jnp.float32, jnp.bfloat16, jnp.int16
ROWS, D = 80, 1152
PAIRS = 20480
SIDE = 16 * ROWS
BUNDLE = 4 * ROWS
OFF4 = (0, 1, 3, 2)
OFF8 = (0, 1, 7, 2, 6, 3, 5, 4)
KEY4 = {off: k for k, off in enumerate(OFF4)}
KEY8 = {off: k for k, off in enumerate(OFF8)}
PIECES = ((0, 32), (32, 16), (48, 32))
FULL = ((0, 1), (2,))
CUT = ((0, 48), (48, 32))
FAR_PARTS = (((0, 32), (32, 48)), (None, (0, 80)), ((0, 80), None), CUT)
COUNT = 224


def normalize(emb):
    full = emb.astype(F32)
    inverse = lax.rsqrt(jnp.sum(full * full, axis=1, keepdims=True) + 1e-06)
    return (full * inverse, inverse)


def back_norm(unit, inverse, direction):
    inner = jnp.sum(unit * direction, axis=1, keepdims=True)
    return inverse * (direction - unit * inner)


class Links:
    def __init__(self, send, recv):
        self.send, self.recv = send, recv
        self.sent, self.open = [], []
        self.used = 0

    def tickets(self, count):
        self.used += count
        assert self.used <= COUNT
        return list(range(self.used - count, self.used))

    def start(self, src, dst, ticket, device):
        copy = pltpu.make_async_remote_copy(
            src_ref=src,
            dst_ref=dst,
            send_sem=self.send.at[len(self.sent)],
            recv_sem=self.recv.at[ticket],
            device_id=device,
            device_id_type=MESH,
        )
        copy.start()
        self.sent.append(copy)
        self.open.append(copy)

    def arrived(self, dst, ticket):
        pltpu.make_async_copy(dst, dst, self.recv.at[ticket]).wait()

    def drain(self):
        for copy in self.open:
            copy.wait_send()
        self.open = []


def by_lanes(body):
    def step(n, _):
        for k in range(3):
            body(pl.ds(pl.multiple_of((n * 3 + k) * 128, 128), 128))
        return 0

    lax.fori_loop(0, D // 384, step, 0)


def widen(q, s, rows, lanes):
    return q[rows, lanes].astype(F32) * s[:, lanes]


def narrow(value, q, s, rows):
    def body(lanes):
        v = value(lanes)
        top = jnp.maximum(jnp.max(jnp.abs(v), axis=0, keepdims=True), 1e-30)
        q[rows, lanes] = jnp.round(v * (32767.0 * pltpu.reciprocal(top, approx=True))).astype(I16)
        s[:, lanes] = top * (1.0 / 32767.0)

    by_lanes(body)


def finish(image_ref, text_ref, loss_part_ref, image_dir_ref, text_dir_ref, loss_ref, grad_image_ref, grad_text_ref):
    loss_ref[...] = loss_part_ref[0:1, 0:1]
    for emb_ref, dir_ref, grad_ref in (
        (image_ref, image_dir_ref, grad_image_ref),
        (text_ref, text_dir_ref, grad_text_ref),
    ):
        unit, inverse = normalize(emb_ref[...])
        grad_ref[...] = back_norm(unit, inverse, dir_ref[...])


def kernel(
    image_ref, text_ref, table_ref, log_scale_ref, bias_ref,
    loss_ref, image_dir_ref, text_dir_ref,
    imgs, txts, slopes, pimg, ptxt,
    mates, mate_rows, mate_all, mate_cols, text_ids, loss_acc,
    far_q, far_s, far_qi, far_si,
    near_q, near_s, near_qi, near_si,
    a_q, a_s, a_qi, a_si,
    sib_q, sib_s, sib_qi, sib_si,
    z_q, z_s, z_qi, z_si,
    loss_x, loss_y, loss_z, loss_c,
    send_sems, recv_sems,
):
    img, txt = lax.axis_index("img"), lax.axis_index("txt")
    x, z_hi = img % 4, img // 4
    core, y, z_lo = txt % 2, (txt // 2) % 4, txt // 8
    z = z_hi * 4 + z_lo

    def dev(x, y, z, core):
        return {"img": (z // 4) * 4 + x, "txt": ((z % 4) * 4 + y) * 2 + core}

    def swap(a, b):
        return a + core * (b - a), b + core * (a - b)

    a, b = swap(x, y)

    def plane(a, b):
        px, py = swap(a % 4, b % 4)
        return dev(px, py, z, core)

    def along_z(k):
        return dev(x, y, (z + k) % 8, core)

    to_a = [plane(a + off, b) for off in OFF4]
    to_b = (plane(a, b + 1), plane(a, b + 3))
    to_z = (along_z(1), along_z(7))
    sibling = dev(x, y, z, 1 - core)
    links = Links(send_sems, recv_sems)

    barrier = pltpu.get_barrier_semaphore()
    partners = [dev((x + k) % 4, y, z, core) for k in (1, 2, 3)]
    partners += [dev(x, (y + k) % 4, z, core) for k in (1, 2, 3)]
    partners += [along_z(k) for k in range(1, 8)] + [sibling]
    for device in partners:
        pl.semaphore_signal(barrier, inc=1, device_id=device, device_id_type=MESH)

    imgs[0:ROWS, :] = normalize(image_ref[...])[0].astype(BF16)
    txts[0:ROWS, :] = normalize(text_ref[...])[0].astype(BF16)
    for k in range(5):
        mates[x, k:k + 1, :] = table_ref[pl.ds(z_lo * 5 + k, 1), :]
    loss_acc[...] = jnp.zeros_like(loss_acc)
    pl.semaphore_wait(barrier, len(partners))

    def img_at(kb, ka):
        return imgs.at[pl.ds((kb * 4 + ka) * ROWS, ROWS), :]

    def txt_at(kz, cc, first=0, count=ROWS):
        return txts.at[pl.ds((kz * 2 + cc) * ROWS + first, count), :]

    ta, ta_far = links.tickets(2), links.tickets(2)
    tb = [links.tickets(4) for _ in range(2)]
    tb_far = [links.tickets(2) for _ in range(4)]
    tz = [[links.tickets(3) for _ in range(4)] for _ in range(2)]
    t_sib = links.tickets(8)
    t_mates = links.tickets(3)

    def b_key(direction):
        return KEY4[3 if direction == 0 else 1]

    def z_key(direction, h):
        return KEY8[-h % 8 if direction == 0 else h]

    def img_part(kb, ka, part):
        return imgs.at[pl.ds((kb * 4 + ka) * ROWS + part[0], part[1]), :]

    def send_a():
        for d in (0, 1):
            links.start(img_at(0, 0), img_at(0, b_key(d)), ta[d], to_a[1 + d])

    def got_a():
        for d in (0, 1):
            links.arrived(img_at(0, b_key(d)), ta[d])
            links.start(img_part(0, b_key(d), CUT[d]), img_part(0, 3, CUT[d]), ta_far[d], to_a[1 + d])

    def got_a_far():
        for d in (0, 1):
            links.arrived(img_part(0, 3, CUT[d]), ta_far[d])

    def send_b(ka):
        for d in (0, 1):
            links.start(img_at(0, ka), img_at(b_key(d), ka), tb[d][ka], to_b[d])

    def got_b(ka):
        for d in (0, 1):
            links.arrived(img_at(b_key(d), ka), tb[d][ka])

    def send_b_far(ka):
        for d in (0, 1):
            part = FAR_PARTS[ka][d]
            if part:
                links.start(img_part(b_key(d), ka, part), img_part(3, ka, part), tb_far[ka][d], to_b[d])

    def got_b_far(ka):
        for d in (0, 1):
            part = FAR_PARTS[ka][d]
            if part:
                links.arrived(img_part(3, ka, part), tb_far[ka][d])

    def send_z(d, h, p):
        first, count = PIECES[p]
        links.start(
            txt_at(z_key(d, h - 1) if h > 1 else 0, 0, first, count),
            txt_at(z_key(d, h), 0, first, count),
            tz[d][h - 1][p],
            to_z[d],
        )

    def got_z(h, p):
        for d in (0, 1):
            if h == 4 and p not in FULL[d]:
                continue
            first, count = PIECES[p]
            links.arrived(txt_at(z_key(d, h), 0, first, count), tz[d][h - 1][p])
            if h < 3 or (h == 3 and p in FULL[d]):
                send_z(d, h + 1, p)


    def send_sib(kz):
        links.start(txt_at(kz, 0), txt_at(kz, 1), t_sib[kz], sibling)

    def got_sib(kz):
        links.arrived(txt_at(kz, 1), t_sib[kz])

    send_a()
    for p in (0, 2, 1):
        for d in (0, 1):
            send_z(d, 1, p)

    column = lax.broadcasted_iota(jnp.int32, (8, SIDE), 1)
    ids = column
    for kz in range(8):
        for cc in (0, 1):
            slot, pz = kz * 2 + cc, (z + OFF8[kz]) % 8
            c = core if cc == 0 else 1 - core
            start = ((((pz % 4) * 4 + y) * 2 + c) * 8 + (pz // 4) * 4 + x) * ROWS
            ids = jnp.where(column >= slot * ROWS, column - slot * ROWS + start, ids)
    text_ids[...] = ids.astype(F32)

    for copy in links.open[0:2]:
        copy.wait_send()
    links.open = links.open[2:]
    send_b(0)
    send_sib(0)
    for k in (1, 2, 3):
        links.start(mates.at[x], mates.at[x], t_mates[k - 1], partners[k - 1])
    got_z(1, 0)
    got_a()
    send_b(1)
    send_b(2)
    got_z(1, 2)
    got_z(1, 1)
    send_sib(1)
    send_sib(2)
    got_a_far()
    send_b(3)
    got_z(2, 0)

    for k in (1, 2, 3):
        links.arrived(mates.at[(x + 4 - k) % 4], t_mates[k - 1])
    mate_rows[...] = jnp.zeros_like(mate_rows)
    for px in range(4):
        mate_rows[px * 8:px * 8 + 5, :] = mates[px, 0:5, :].astype(F32)
    turned = mate_rows[...].T
    for px in range(4):
        for k in range(5):
            mate_all[px, k * 128:(k + 1) * 128, :] = jnp.broadcast_to(
                turned[:, px * 8 + k:px * 8 + k + 1], (128, 128)
            )
    for kb in range(4):
        for ka in range(4):
            px, py = swap((a + OFF4[ka]) % 4, (b + OFF4[kb]) % 4)
            start = pl.multiple_of((2 * py + core) * ROWS, 16)
            mate_cols[(kb * 4 + ka) * ROWS:(kb * 4 + ka + 1) * ROWS, :] = mate_all[px, pl.ds(start, ROWS), :]

    scale = jnp.exp(log_scale_ref[...])
    to_log2 = scale * math.log2(math.e)
    shift = bias_ref[...] * math.log2(math.e)

    def tile(kb, first, count):
        rows = pl.ds(kb * BUNDLE if isinstance(kb, int) else pl.multiple_of(kb * BUNDLE, BUNDLE), BUNDLE)
        cols = pl.ds(first, count)
        cosine = lax.dot_general(
            imgs[rows, :], txts[cols, :], (((1,), (1,)), ((), ())), preferred_element_type=F32
        )
        logits = cosine * to_log2 + shift
        e = jnp.exp2(logits)
        u = 1.0 + e
        r = pltpu.reciprocal(u, approx=True)
        mate = mate_cols[rows, :]
        positive = jnp.concatenate([mate] * (count // 128), axis=1) == text_ids[0:1, cols]
        slopes[rows, cols] = jnp.where(positive, -r, e * r).astype(BF16)
        lost = (e - (u - 1.0)) * r
        paired = jnp.where(positive, logits, 0.0)
        product = u[0:80] * u[80:160] * u[160:240] * u[240:320]
        total = jnp.log(product).reshape(10, 8, count).sum(0)
        total += lost.reshape(40, 8, count).sum(0) - paired.reshape(40, 8, count).sum(0) * math.log(2.0)
        folded = total[:, 0:128]
        for k in range(128, count, 128):
            folded = folded + total[:, k:k + 128]
        loss_acc[...] += folded

    def text_part(first, count, low, high):
        rows, depth = pl.ds(first, count), pl.ds(low, high - low)
        part = lax.dot_general(
            slopes[depth, rows], imgs[depth, :], (((0,), (0,)), ((), ())), preferred_element_type=F32
        )
        if low:
            ptxt[rows, :] += part
        else:
            ptxt[rows, :] = part

    def tiles(low, high, first, count):
        def step(kb, _):
            tile(kb, first, count)
            return 0

        lax.fori_loop(low, high, step, 0)

    got_z(2, 2)
    got_z(2, 1)
    send_sib(3)
    send_sib(4)
    got_sib(0)
    got_sib(1)
    tile(0, 0, 256)
    got_b(1)
    send_b_far(1)
    got_b(2)
    send_b_far(2)
    got_b(0)
    send_b_far(0)
    got_z(3, 0)
    got_z(3, 2)
    got_z(3, 1)
    send_sib(5)
    send_sib(6)
    got_sib(2)
    got_sib(3)
    got_sib(4)
    tile(0, 256, 512)
    got_b(3)
    send_b_far(3)
    tiles(1, 3, 0, 768)
    for p in (0, 2, 1):
        got_z(4, p)
    send_sib(7)
    got_sib(5)
    got_sib(6)
    got_sib(7)
    tiles(0, 3, 768, 512)
    text_part(768, 512, 0, 960)
    for ka in (2, 1, 0, 3):
        got_b_far(ka)
    tile(3, 0, 1280)

    lx, ly, lz, lc = links.tickets(3), links.tickets(3), links.tickets(7), links.tickets(1)

    def share(buffer, me, size, tickets, devices):
        for k in range(1, size):
            links.start(buffer.at[me], buffer.at[me], tickets[k - 1], devices[k - 1])

    def gathered(buffer, me, size, tickets):
        for k in range(1, size):
            links.arrived(buffer.at[(me + size - k) % size], tickets[k - 1])
        total = buffer[0]
        for k in range(1, size):
            total = total + buffer[k]
        return total

    def image_part(kb):
        rows = pl.ds(kb * BUNDLE, BUNDLE)
        pimg[rows, :] = jnp.dot(slopes[rows, :], txts[...], preferred_element_type=F32)

    whole = pl.ds(0, ROWS)

    def send_pair(q, s, q_in, s_in, tickets, device):
        links.start(q, q_in, tickets[0], device)
        links.start(s, s_in, tickets[1], device)

    def got_pair(q_in, s_in, tickets):
        links.arrived(q_in, tickets[0])
        links.arrived(s_in, tickets[1])

    def img_rows(kb, ka):
        return pl.ds((kb * 4 + ka) * ROWS, ROWS)

    FAR = ((3, 2), (1, 0))
    u_far = {ka: links.tickets(2) for ka in range(4)}
    u_near = [{ka: links.tickets(2) for ka in range(4)} for _ in range(2)]
    u_a = {ka: links.tickets(2) for ka in (1, 2, 3)}
    u_sib = [links.tickets(2) for _ in range(8)]
    u_z = [[[links.tickets(2) for _ in range(3)] for _ in range(4)] for _ in range(2)]

    def send_far():
        for n in (0, 1):
            for d in (0, 1):
                ka = FAR[d][n]
                narrow(lambda lanes: pimg[img_rows(3, ka), lanes], far_q.at[ka], far_s.at[ka], whole)
                send_pair(far_q.at[ka], far_s.at[ka], far_qi.at[ka], far_si.at[ka], u_far[ka], to_b[d])

    def send_near(d, ka):
        kb = KEY4[1 if d == 0 else 3]
        added = ka in FAR[d]
        if added:
            got_pair(far_qi.at[ka], far_si.at[ka], u_far[ka])

        def value(lanes):
            v = pimg[img_rows(kb, ka), lanes]
            return v + widen(far_qi.at[ka], far_si.at[ka], whole, lanes) if added else v

        n = d * 4 + ka
        narrow(value, near_q.at[n], near_s.at[n], whole)
        send_pair(near_q.at[n], near_s.at[n], near_qi.at[n], near_si.at[n], u_near[d][ka], to_b[d])

    def fold(ka):
        for d in (0, 1):
            got_pair(near_qi.at[d * 4 + ka], near_si.at[d * 4 + ka], u_near[d][ka])

        def value(lanes):
            v = pimg[img_rows(0, ka), lanes]
            return v + widen(near_qi.at[ka], near_si.at[ka], whole, lanes) + widen(
                near_qi.at[4 + ka], near_si.at[4 + ka], whole, lanes
            )

        if ka:
            narrow(value, a_q.at[ka], a_s.at[ka], whole)
            send_pair(a_q.at[ka], a_s.at[ka], a_qi.at[ka], a_si.at[ka], u_a[ka], to_a[ka])
        else:
            def body(lanes):
                pimg[0:ROWS, lanes] = value(lanes)

            by_lanes(body)

    def swap_text(kz):
        rows = pl.ds((kz * 2 + 1) * ROWS, ROWS)
        narrow(lambda lanes: ptxt[rows, lanes], sib_q.at[kz], sib_s.at[kz], whole)
        send_pair(sib_q.at[kz], sib_s.at[kz], sib_qi.at[kz], sib_si.at[kz], u_sib[kz], sibling)

    def got_swap(kz):
        got_pair(sib_qi.at[kz], sib_si.at[kz], u_sib[kz])

    def z_piece(buffer, d, r, p):
        return buffer.at[d * 4 + r - 1, pl.ds(*PIECES[p]), :]

    def z_step(d, r, p):
        return (d * 4 + r - 1) * 3 + p

    def got_zsum(d, r, p):
        got_pair(z_piece(z_qi, d, r, p), z_si.at[z_step(d, r, p)], u_z[d][r - 1][p])

    def send_zsum(d, r, p):
        first, count = PIECES[p]
        kz = KEY8[r % 8 if d == 0 else -r % 8]
        added = r < 3 or (r == 3 and p in FULL[d])
        if added:
            got_zsum(d, r + 1, p)
        here = pl.ds(first, count)

        def value(lanes):
            v = ptxt[pl.ds(kz * 2 * ROWS + first, count), lanes] + widen(sib_qi.at[kz], sib_si.at[kz], here, lanes)
            if added:
                v = v + widen(z_qi.at[d * 4 + r], z_si.at[z_step(d, r + 1, p)], here, lanes)
            return v

        n = z_step(d, r, p)
        narrow(value, z_q.at[d * 4 + r - 1], z_s.at[n], here)
        send_pair(
            z_piece(z_q, d, r, p), z_s.at[n], z_piece(z_qi, d, r, p), z_si.at[n], u_z[d][r - 1][p], to_z[d]
        )

    part = jnp.sum(jnp.sum(loss_acc[...], axis=0, keepdims=True), axis=1, keepdims=True)
    loss_x[x] = jnp.broadcast_to(part, (8, 128))
    share(loss_x, x, 4, lx, partners[0:3])
    text_part(768, 512, 960, 1280)
    for kz in (7, 5, 6):
        swap_text(kz)
    image_part(3)
    send_far()
    got_swap(7)
    for p, d in ((0, 0), (2, 1), (1, 0)):
        send_zsum(d, 4, p)
    got_swap(5)
    got_swap(6)
    for p, d in ((2, 0), (0, 1), (1, 1)):
        send_zsum(d, 3, p)
    image_part(1)
    send_near(0, 1)
    image_part(2)
    send_near(1, 3)
    loss_y[y] = gathered(loss_x, x, 4, lx)
    share(loss_y, y, 4, ly, partners[3:6])
    send_near(0, 3)
    send_near(1, 1)
    for p, d in ((0, 0), (2, 1), (1, 0)):
        send_zsum(d, 3, p)
    send_near(1, 2)
    send_near(0, 2)
    text_part(256, 512, 0, 1280)
    for kz in (3, 4, 2):
        swap_text(kz)
    send_near(0, 0)
    send_near(1, 0)
    got_swap(3)
    got_swap(4)
    for p, d in ((2, 0), (0, 1), (1, 1), (0, 0), (2, 1), (1, 0)):
        send_zsum(d, 2, p)
    image_part(0)
    fold(3)
    fold(1)
    text_part(0, 256, 0, 1280)
    for kz in (1, 0):
        swap_text(kz)
    loss_z[z] = gathered(loss_y, y, 4, ly)
    share(loss_z, z, 8, lz, partners[6:13])
    fold(2)
    got_swap(1)
    got_swap(2)
    for p, d in ((2, 0), (0, 1), (1, 1), (0, 0), (2, 1), (1, 0)):
        send_zsum(d, 1, p)
    fold(0)
    loss_c[core] = gathered(loss_z, z, 8, lz)
    share(loss_c, core, 2, lc, [sibling])
    got_swap(0)

    for ka in (1, 2, 3):
        got_pair(a_qi.at[ka], a_si.at[ka], u_a[ka])

    def image_sum(lanes):
        v = pimg[0:ROWS, lanes]
        for ka in (1, 2, 3):
            v = v + widen(a_qi.at[ka], a_si.at[ka], whole, lanes)
        image_dir_ref[:, lanes] = v * scale

    by_lanes(image_sum)

    for p, d in ((2, 0), (0, 1), (1, 1), (0, 0), (2, 1), (1, 0)):
        got_zsum(d, 1, p)

    def text_sum(lanes):
        for p, (first, count) in enumerate(PIECES):
            here = pl.ds(first, count)
            v = ptxt[here, lanes] + widen(sib_qi.at[0], sib_si.at[0], here, lanes)
            for d in (0, 1):
                v = v + widen(z_qi.at[d * 4], z_si.at[z_step(d, 1, p)], here, lanes)
            text_dir_ref[here, lanes] = v * scale

    by_lanes(text_sum)
    loss_ref[...] = gathered(loss_c, core, 2, lc) * (1.0 / PAIRS)
    links.drain()


def on_device(image_emb, text_emb, partner, log_scale, bias):
    vmem = pl.BlockSpec(memory_space=pltpu.VMEM)

    def messages(count):
        return [pltpu.VMEM((count, ROWS, D), I16), pltpu.VMEM((count, 1, D), F32)] * 2

    loss, image_dir, text_dir = pl.pallas_call(
        kernel,
        out_shape=(
            jax.ShapeDtypeStruct((8, 128), F32),
            jax.ShapeDtypeStruct((ROWS, D), F32),
            jax.ShapeDtypeStruct((ROWS, D), F32),
        ),
        in_specs=[vmem] * 5,
        out_specs=(vmem, vmem, vmem),
        scratch_shapes=[
            pltpu.VMEM((SIDE, D), BF16),
            pltpu.VMEM((SIDE, D), BF16),
            pltpu.VMEM((SIDE, SIDE), BF16),
            pltpu.VMEM((SIDE, D), F32),
            pltpu.VMEM((SIDE, D), F32),
            pltpu.VMEM((4, 8, 128), jnp.int32),
            pltpu.VMEM((128, 128), F32),
            pltpu.VMEM((4, 640, 128), F32),
            pltpu.VMEM((SIDE, 128), F32),
            pltpu.VMEM((8, SIDE), F32),
            pltpu.VMEM((8, 128), F32),
            *messages(4),
            *messages(8),
            *messages(4),
            *messages(8),
            *[pltpu.VMEM((8, ROWS, D), I16), pltpu.VMEM((24, 1, D), F32)] * 2,
            pltpu.VMEM((4, 8, 128), F32),
            pltpu.VMEM((4, 8, 128), F32),
            pltpu.VMEM((8, 8, 128), F32),
            pltpu.VMEM((2, 8, 128), F32),
            pltpu.SemaphoreType.DMA((COUNT,)),
            pltpu.SemaphoreType.DMA((COUNT,)),
        ],
        compiler_params=pltpu.CompilerParams(
            collective_id=0, has_side_effects=True, vmem_limit_bytes=60 * 1024 * 1024
        ),
    )(image_emb, text_emb, partner.reshape(20, 128), log_scale.reshape(1, 1), bias.reshape(1, 1))
    loss, grad_image, grad_text = pl.pallas_call(
        finish,
        out_shape=(
            jax.ShapeDtypeStruct((1, 1), F32),
            jax.ShapeDtypeStruct((ROWS, D), F32),
            jax.ShapeDtypeStruct((ROWS, D), F32),
        ),
        in_specs=[vmem] * 5,
        out_specs=(vmem, vmem, vmem),
    )(image_emb, text_emb, loss, image_dir, text_dir)
    return (loss.reshape(1), grad_image, grad_text)


def solution(mesh):
    return jax.shard_map(
        on_device,
        mesh=mesh,
        in_specs=(P(("img", "txt"), None), P(("txt", "img"), None), P("img"), P(), P()),
        out_specs=(P(), P(("img", "txt"), None), P(("txt", "img"), None)),
        check_vma=False,
    )
```

```python
import math

import jax
import jax.numpy as jnp
from jax import lax
from jax.experimental import pallas as pl
from jax.experimental.pallas import tpu as pltpu
from jax.sharding import PartitionSpec as P

MESH = pl.DeviceIdType.MESH
F32, BF16, I16 = jnp.float32, jnp.bfloat16, jnp.int16
ROWS, D = 80, 1152
PAIRS = 20480
SIDE = 16 * ROWS
BUNDLE = 4 * ROWS
OFF4 = (0, 1, 3, 2)
OFF8 = (0, 1, 7, 2, 6, 3, 5, 4)
KEY4 = {off: k for k, off in enumerate(OFF4)}
KEY8 = {off: k for k, off in enumerate(OFF8)}
PIECES = ((0, 48), (48, 32))
FULL = ((0,), (1,))
CUT = ((0, 48), (48, 32))
FAR_PARTS = (((0, 32), (32, 48)), (None, (0, 80)), ((0, 80), None), CUT)
COUNT = 224


def normalize(emb):
    full = emb.astype(F32)
    inverse = lax.rsqrt(jnp.sum(full * full, axis=1, keepdims=True) + 1e-06)
    return (full * inverse, inverse)


def back_norm(unit, inverse, direction):
    inner = jnp.sum(unit * direction, axis=1, keepdims=True)
    return inverse * (direction - unit * inner)


class Links:
    def __init__(self, send, recv):
        self.send, self.recv = send, recv
        self.sent, self.open = [], []
        self.used = 0

    def tickets(self, count):
        self.used += count
        assert self.used <= COUNT
        return list(range(self.used - count, self.used))

    def start(self, src, dst, ticket, device):
        copy = pltpu.make_async_remote_copy(
            src_ref=src,
            dst_ref=dst,
            send_sem=self.send.at[len(self.sent)],
            recv_sem=self.recv.at[ticket],
            device_id=device,
            device_id_type=MESH,
        )
        copy.start()
        self.sent.append(copy)
        self.open.append(copy)

    def arrived(self, dst, ticket):
        pltpu.make_async_copy(dst, dst, self.recv.at[ticket]).wait()

    def drain(self):
        for copy in self.open:
            copy.wait_send()
        self.open = []


def by_lanes(body):
    def step(n, _):
        for k in range(3):
            body(pl.ds(pl.multiple_of((n * 3 + k) * 128, 128), 128))
        return 0

    lax.fori_loop(0, D // 384, step, 0)


def widen(q, s, rows, lanes):
    return q[rows, lanes].astype(F32) * s[:, lanes]


def narrow(items):
    def body(lanes):
        for value, q, s, rows in items:
            v = value(lanes)
            top = jnp.maximum(jnp.max(jnp.abs(v), axis=0, keepdims=True), 1e-30)
            q[rows, lanes] = jnp.round(v * (32767.0 * pltpu.reciprocal(top, approx=True))).astype(I16)
            s[:, lanes] = top * (1.0 / 32767.0)

    by_lanes(body)


def finish(image_ref, text_ref, loss_part_ref, image_dir_ref, text_dir_ref, loss_ref, grad_image_ref, grad_text_ref):
    loss_ref[...] = loss_part_ref[0:1, 0:1]
    for emb_ref, dir_ref, grad_ref in (
        (image_ref, image_dir_ref, grad_image_ref),
        (text_ref, text_dir_ref, grad_text_ref),
    ):
        unit, inverse = normalize(emb_ref[...])
        grad_ref[...] = back_norm(unit, inverse, dir_ref[...])


def kernel(
    image_hbm, text_hbm, table_hbm, log_scale_hbm, bias_hbm,
    loss_ref, image_dir_ref, text_dir_ref,
    image_ref, text_ref, table_ref, log_scale_ref, bias_ref, load_sems,
    imgs, txts, slopes, pimg, ptxt,
    mates, mate_rows, mate_all, mate_cols, text_ids, loss_acc,
    far_q, far_s, far_qi, far_si,
    near_q, near_s, near_qi, near_si,
    a_q, a_s, a_qi, a_si,
    sib_q, sib_s, sib_qi, sib_si,
    z_q, z_s, z_qi, z_si,
    loss_x, loss_y, loss_z, loss_c,
    send_sems, recv_sems,
):
    img, txt = lax.axis_index("img"), lax.axis_index("txt")
    x, z_hi = img % 4, img // 4
    core, y, z_lo = txt % 2, (txt // 2) % 4, txt // 8
    z = z_hi * 4 + z_lo

    def dev(x, y, z, core):
        return {"img": (z // 4) * 4 + x, "txt": ((z % 4) * 4 + y) * 2 + core}

    def swap(a, b):
        return a + core * (b - a), b + core * (a - b)

    a, b = swap(x, y)

    def plane(a, b):
        px, py = swap(a % 4, b % 4)
        return dev(px, py, z, core)

    def along_z(k):
        return dev(x, y, (z + k) % 8, core)

    to_a = [plane(a + off, b) for off in OFF4]
    to_b = (plane(a, b + 1), plane(a, b + 3))
    to_z = (along_z(1), along_z(7))
    sibling = dev(x, y, z, 1 - core)
    links = Links(send_sems, recv_sems)

    barrier = pltpu.get_barrier_semaphore()
    partners = [dev((x + k) % 4, y, z, core) for k in (1, 2, 3)]
    partners += [dev(x, (y + k) % 4, z, core) for k in (1, 2, 3)]
    partners += [along_z(k) for k in range(1, 8)] + [sibling]
    for device in partners:
        pl.semaphore_signal(barrier, inc=1, device_id=device, device_id_type=MESH)

    loads = [
        pltpu.make_async_copy(src, dst, load_sems.at[k])
        for k, (src, dst) in enumerate((
            (image_hbm, image_ref), (text_hbm, text_ref), (table_hbm, table_ref),
            (log_scale_hbm, log_scale_ref), (bias_hbm, bias_ref),
        ))
    ]
    for load in loads:
        load.start()
    loads[0].wait()
    imgs[0:ROWS, :] = normalize(image_ref[...])[0].astype(BF16)
    loads[1].wait()
    txts[0:ROWS, :] = normalize(text_ref[...])[0].astype(BF16)
    loads[2].wait()
    for k in range(5):
        mates[x, k:k + 1, :] = table_ref[pl.ds(z_lo * 5 + k, 1), :]
    loss_acc[...] = jnp.zeros_like(loss_acc)
    pl.semaphore_wait(barrier, len(partners))

    def img_at(kb, ka):
        return imgs.at[pl.ds((kb * 4 + ka) * ROWS, ROWS), :]

    def txt_at(kz, cc, first=0, count=ROWS):
        return txts.at[pl.ds((kz * 2 + cc) * ROWS + first, count), :]

    ta, ta_far = links.tickets(2), links.tickets(2)
    tb = [links.tickets(4) for _ in range(2)]
    tb_far = [links.tickets(2) for _ in range(4)]
    tz = [[links.tickets(2) for _ in range(4)] for _ in range(2)]
    t_sib = links.tickets(8)
    t_mates = links.tickets(3)

    def b_key(direction):
        return KEY4[3 if direction == 0 else 1]

    def z_key(direction, h):
        return KEY8[-h % 8 if direction == 0 else h]

    def img_part(kb, ka, part):
        return imgs.at[pl.ds((kb * 4 + ka) * ROWS + part[0], part[1]), :]

    def send_a():
        for d in (0, 1):
            links.start(img_at(0, 0), img_at(0, b_key(d)), ta[d], to_a[1 + d])

    def got_a():
        for d in (0, 1):
            links.arrived(img_at(0, b_key(d)), ta[d])
            links.start(img_part(0, b_key(d), CUT[d]), img_part(0, 3, CUT[d]), ta_far[d], to_a[1 + d])

    def got_a_far():
        for d in (0, 1):
            links.arrived(img_part(0, 3, CUT[d]), ta_far[d])

    def send_b(ka):
        for d in (0, 1):
            links.start(img_at(0, ka), img_at(b_key(d), ka), tb[d][ka], to_b[d])

    def got_b(ka):
        for d in (0, 1):
            links.arrived(img_at(b_key(d), ka), tb[d][ka])

    def send_b_far(ka):
        for d in (0, 1):
            part = FAR_PARTS[ka][d]
            if part:
                links.start(img_part(b_key(d), ka, part), img_part(3, ka, part), tb_far[ka][d], to_b[d])

    def got_b_far(ka):
        for d in (0, 1):
            part = FAR_PARTS[ka][d]
            if part:
                links.arrived(img_part(3, ka, part), tb_far[ka][d])

    def send_z(d, h, p):
        first, count = PIECES[p]
        links.start(
            txt_at(z_key(d, h - 1) if h > 1 else 0, 0, first, count),
            txt_at(z_key(d, h), 0, first, count),
            tz[d][h - 1][p],
            to_z[d],
        )

    def got_z(h, p):
        for d in (0, 1):
            if h == 4 and p not in FULL[d]:
                continue
            first, count = PIECES[p]
            links.arrived(txt_at(z_key(d, h), 0, first, count), tz[d][h - 1][p])
            if h < 3 or (h == 3 and p in FULL[d]):
                send_z(d, h + 1, p)


    def send_sib(kz):
        links.start(txt_at(kz, 0), txt_at(kz, 1), t_sib[kz], sibling)

    def got_sib(kz):
        links.arrived(txt_at(kz, 1), t_sib[kz])

    send_a()
    for p in (0, 1):
        for d in (0, 1):
            send_z(d, 1, p)

    column = lax.broadcasted_iota(jnp.int32, (8, SIDE), 1)
    ids = column
    for kz in range(8):
        for cc in (0, 1):
            slot, pz = kz * 2 + cc, (z + OFF8[kz]) % 8
            c = core if cc == 0 else 1 - core
            start = ((((pz % 4) * 4 + y) * 2 + c) * 8 + (pz // 4) * 4 + x) * ROWS
            ids = jnp.where(column >= slot * ROWS, column - slot * ROWS + start, ids)
    text_ids[...] = ids.astype(F32)

    for copy in links.open[0:2]:
        copy.wait_send()
    links.open = links.open[2:]
    send_b(0)
    send_sib(0)
    for k in (1, 2, 3):
        links.start(mates.at[x], mates.at[x], t_mates[k - 1], partners[k - 1])
    got_z(1, 0)
    got_a()
    send_b(1)
    send_b(2)
    for k in (1, 2, 3):
        links.arrived(mates.at[(x + 4 - k) % 4], t_mates[k - 1])
    mate_rows[...] = jnp.zeros_like(mate_rows)
    for px in range(4):
        mate_rows[px * 8:px * 8 + 5, :] = mates[px, 0:5, :].astype(F32)
    turned = mate_rows[...].T
    for px in range(4):
        for k in range(5):
            mate_all[px, k * 128:(k + 1) * 128, :] = jnp.broadcast_to(
                turned[:, px * 8 + k:px * 8 + k + 1], (128, 128)
            )
    for kb in range(4):
        for ka in range(4):
            px, py = swap((a + OFF4[ka]) % 4, (b + OFF4[kb]) % 4)
            start = pl.multiple_of((2 * py + core) * ROWS, 16)
            mate_cols[(kb * 4 + ka) * ROWS:(kb * 4 + ka + 1) * ROWS, :] = mate_all[px, pl.ds(start, ROWS), :]

    got_z(1, 1)
    send_sib(1)
    send_sib(2)
    got_a_far()
    send_b(3)
    got_z(2, 0)

    loads[3].wait()
    loads[4].wait()
    scale = jnp.exp(jnp.full((1, 1), log_scale_ref[0], F32))
    to_log2 = scale * math.log2(math.e)
    shift = jnp.full((1, 1), bias_ref[0] * math.log2(math.e), F32)

    def tile(kb, top, height, first, count):
        rows = pl.ds(kb * BUNDLE + top if isinstance(kb, int) else pl.multiple_of(kb * BUNDLE + top, 16), height)
        cols = pl.ds(first, count)
        cosine = lax.dot_general(
            imgs[rows, :], txts[cols, :], (((1,), (1,)), ((), ())), preferred_element_type=F32
        )
        logits = cosine * to_log2 + shift
        e = jnp.exp2(logits)
        u = 1.0 + e
        r = pltpu.reciprocal(u, approx=True)
        mate = mate_cols[rows, :]
        positive = jnp.concatenate([mate] * (count // 128), axis=1) == text_ids[0:1, cols]
        slopes[rows, cols] = jnp.where(positive, -r, e * r).astype(BF16)
        paired = jnp.where(positive, logits, 0.0)
        grown = [e[k:k + ROWS] for k in range(0, height, ROWS)]
        while len(grown) > 1:
            first_e, second_e, *others = grown
            grown = [*others, first_e + second_e + first_e * second_e]
        over = 1.0 + grown[0]
        lost = jnp.log(over) + (grown[0] - (over - 1.0)) * pltpu.reciprocal(over, approx=True)
        total = lost.reshape(10, 8, count).sum(0)
        total -= paired.reshape(height // 8, 8, count).sum(0) * math.log(2.0)
        folded = total[:, 0:128]
        for k in range(128, count, 128):
            folded = folded + total[:, k:k + 128]
        loss_acc[...] += folded

    def text_part(first, count, low=0, high=SIDE):
        rows, depth = pl.ds(first, count), pl.ds(low, high - low)
        part = lax.dot_general(
            slopes[depth, rows], imgs[depth, :], (((0,), (0,)), ((), ())), preferred_element_type=F32
        )
        if low:
            ptxt[rows, :] += part
        else:
            ptxt[rows, :] = part

    def tiles(low, high, top, height, first, count):
        def step(kb, _):
            tile(kb, top, height, first, count)
            return 0

        lax.fori_loop(low, high, step, 0)

    got_z(2, 1)
    send_sib(3)
    send_sib(4)
    got_b(1)
    send_b_far(1)
    got_b(2)
    send_b_far(2)
    got_b(0)
    send_b_far(0)
    for kz in (0, 1, 2, 3, 4):
        got_sib(kz)
    tile(0, 0, BUNDLE, 0, 768)
    got_z(3, 0)
    got_z(3, 1)
    send_sib(5)
    send_sib(6)
    got_b(3)
    send_b_far(3)
    tiles(1, 3, 0, BUNDLE, 0, 768)
    text_part(0, 384, 0, 960)
    for p in (0, 1):
        got_z(4, p)
    send_sib(7)
    text_part(384, 384, 0, 960)
    got_sib(5)
    got_sib(6)
    got_sib(7)
    tiles(0, 3, 0, BUNDLE, 768, 512)

    lx, ly, lz, lc = links.tickets(3), links.tickets(3), links.tickets(7), links.tickets(1)

    def share(buffer, me, size, tickets, devices):
        for k in range(1, size):
            links.start(buffer.at[me], buffer.at[me], tickets[k - 1], devices[k - 1])

    def gathered(buffer, me, size, tickets):
        for k in range(1, size):
            links.arrived(buffer.at[(me + size - k) % size], tickets[k - 1])
        total = buffer[0]
        for k in range(1, size):
            total = total + buffer[k]
        return total

    def image_part(kb):
        rows = pl.ds(kb * BUNDLE, BUNDLE)
        pimg[rows, :] = jnp.dot(slopes[rows, :], txts[...], preferred_element_type=F32)

    whole = pl.ds(0, ROWS)

    def send_pair(q, s, q_in, s_in, tickets, device):
        links.start(q, q_in, tickets[0], device)
        links.start(s, s_in, tickets[1], device)

    def got_pair(q_in, s_in, tickets):
        links.arrived(q_in, tickets[0])
        links.arrived(s_in, tickets[1])

    def img_rows(kb, ka):
        return pl.ds((kb * 4 + ka) * ROWS, ROWS)

    FAR = ((3, 2), (1, 0))
    u_far = {ka: links.tickets(2) for ka in range(4)}
    u_near = [{ka: links.tickets(2) for ka in range(4)} for _ in range(2)]
    u_a = {ka: links.tickets(2) for ka in (1, 2, 3)}
    u_sib = [links.tickets(2) for _ in range(8)]
    u_z = [[[links.tickets(2) for _ in range(2)] for _ in range(4)] for _ in range(2)]

    def send_far(n):
        items = []
        for d in (0, 1):
            rows = img_rows(3, FAR[d][n])
            items.append((lambda lanes, rows=rows: pimg[rows, lanes], far_q.at[FAR[d][n]], far_s.at[FAR[d][n]], whole))
        narrow(items)
        for d in (0, 1):
            ka = FAR[d][n]
            send_pair(far_q.at[ka], far_s.at[ka], far_qi.at[ka], far_si.at[ka], u_far[ka], to_b[d])

    sent_near = []

    def send_near(pairs):
        items = []
        for d, ka in pairs:
            rows = img_rows(KEY4[1 if d == 0 else 3], ka)
            if ka in FAR[d]:
                got_pair(far_qi.at[ka], far_si.at[ka], u_far[ka])

            def value(lanes, d=d, ka=ka, rows=rows):
                v = pimg[rows, lanes]
                return v + widen(far_qi.at[ka], far_si.at[ka], whole, lanes) if ka in FAR[d] else v

            items.append((value, near_q.at[d * 4 + ka], near_s.at[d * 4 + ka], whole))
        narrow(items)
        for d in (0, 1):
            kas = [ka for e, ka in pairs if e == d]
            if kas:
                n = pl.ds(d * 4 + min(kas), len(kas))
                send_pair(near_q.at[n], near_s.at[n], near_qi.at[n], near_si.at[n], u_near[d][min(kas)], to_b[d])
                sent_near.append((d, tuple(kas)))

    def fold(ka):
        for d, kas in list(sent_near):
            if ka in kas:
                n = pl.ds(d * 4 + min(kas), len(kas))
                got_pair(near_qi.at[n], near_si.at[n], u_near[d][min(kas)])
                sent_near.remove((d, kas))

        def value(lanes):
            v = pimg[img_rows(0, ka), lanes]
            return v + widen(near_qi.at[ka], near_si.at[ka], whole, lanes) + widen(
                near_qi.at[4 + ka], near_si.at[4 + ka], whole, lanes
            )

        if ka:
            narrow([(value, a_q.at[ka], a_s.at[ka], whole)])
            send_pair(a_q.at[ka], a_s.at[ka], a_qi.at[ka], a_si.at[ka], u_a[ka], to_a[ka])
        else:
            def body(lanes):
                pimg[0:ROWS, lanes] = value(lanes)

            by_lanes(body)

    def swap_text(keys):
        items = []
        for kz in keys:
            rows = pl.ds((kz * 2 + 1) * ROWS, ROWS)
            items.append((lambda lanes, rows=rows: ptxt[rows, lanes], sib_q.at[kz], sib_s.at[kz], whole))
        narrow(items)
        for kz in keys:
            send_pair(sib_q.at[kz], sib_s.at[kz], sib_qi.at[kz], sib_si.at[kz], u_sib[kz], sibling)

    def got_swap(kz):
        got_pair(sib_qi.at[kz], sib_si.at[kz], u_sib[kz])

    def z_piece(buffer, d, r, p):
        return buffer.at[d * 4 + r - 1, pl.ds(*PIECES[p]), :]

    def z_step(d, r, p):
        return (d * 4 + r - 1) * 2 + p

    def got_zsum(d, r, p):
        got_pair(z_piece(z_qi, d, r, p), z_si.at[z_step(d, r, p)], u_z[d][r - 1][p])

    LONG, SHORT = ((0, 0), (1, 1)), ((1, 0), (0, 1))

    def send_zsum(r, chains):
        items = []
        for p, d in chains:
            first, count = PIECES[p]
            kz = KEY8[r % 8 if d == 0 else -r % 8]
            added = r < 3 or (r == 3 and p in FULL[d])
            if added:
                got_zsum(d, r + 1, p)
            here = pl.ds(first, count)

            def value(lanes, d=d, p=p, first=first, count=count, kz=kz, added=added, here=here):
                v = ptxt[pl.ds(kz * 2 * ROWS + first, count), lanes] + widen(sib_qi.at[kz], sib_si.at[kz], here, lanes)
                if added:
                    v = v + widen(z_qi.at[d * 4 + r], z_si.at[z_step(d, r + 1, p)], here, lanes)
                return v

            items.append((value, z_q.at[d * 4 + r - 1], z_s.at[z_step(d, r, p)], here))
        narrow(items)
        for p, d in chains:
            n = z_step(d, r, p)
            send_pair(
                z_piece(z_q, d, r, p), z_s.at[n], z_piece(z_qi, d, r, p), z_si.at[n], u_z[d][r - 1][p], to_z[d]
            )

    for ka in (2, 1, 0, 3):
        got_b_far(ka)
    tile(3, 0, BUNDLE, 0, SIDE)
    text_part(768, 512)
    swap_text((7, 5, 6))
    image_part(3)
    send_far(0)
    send_far(1)
    got_swap(7)
    send_zsum(4, LONG)
    got_swap(5)
    got_swap(6)
    send_zsum(3, SHORT)
    part = jnp.sum(jnp.sum(loss_acc[...], axis=0, keepdims=True), axis=1, keepdims=True)
    loss_x[x] = jnp.broadcast_to(part, (8, 128))
    share(loss_x, x, 4, lx, partners[0:3])
    image_part(1)
    send_near(((0, 1), (0, 0)))
    image_part(2)
    send_near(((1, 3), (1, 2)))
    text_part(0, 768, 960, SIDE)
    swap_text((3, 4, 2, 1, 0))
    image_part(0)
    send_zsum(3, LONG)
    send_near(((0, 3), (1, 1)))
    loss_y[y] = gathered(loss_x, x, 4, lx)
    share(loss_y, y, 4, ly, partners[3:6])
    got_swap(3)
    got_swap(4)
    send_zsum(2, SHORT)
    send_near(((0, 2), (1, 0)))
    fold(3)
    send_zsum(2, LONG)
    loss_z[z] = gathered(loss_y, y, 4, ly)
    share(loss_z, z, 8, lz, partners[6:13])
    got_swap(1)
    got_swap(2)
    send_zsum(1, SHORT)
    fold(1)
    fold(2)
    send_zsum(1, LONG)
    fold(0)
    loss_c[core] = gathered(loss_z, z, 8, lz)
    share(loss_c, core, 2, lc, [sibling])
    got_swap(0)

    for ka in (1, 2, 3):
        got_pair(a_qi.at[ka], a_si.at[ka], u_a[ka])

    def image_sum(lanes):
        v = pimg[0:ROWS, lanes]
        for ka in (1, 2, 3):
            v = v + widen(a_qi.at[ka], a_si.at[ka], whole, lanes)
        image_dir_ref[:, lanes] = v * scale

    by_lanes(image_sum)

    for p, d in (*SHORT, *LONG):
        got_zsum(d, 1, p)

    def text_sum(lanes):
        for p, (first, count) in enumerate(PIECES):
            here = pl.ds(first, count)
            v = ptxt[here, lanes] + widen(sib_qi.at[0], sib_si.at[0], here, lanes)
            for d in (0, 1):
                v = v + widen(z_qi.at[d * 4], z_si.at[z_step(d, 1, p)], here, lanes)
            text_dir_ref[here, lanes] = v * scale

    by_lanes(text_sum)
    loss_ref[...] = gathered(loss_c, core, 2, lc) * (1.0 / PAIRS)
    links.drain()


def on_device(image_emb, text_emb, partner, log_scale, bias):
    vmem = pl.BlockSpec(memory_space=pltpu.VMEM)

    def messages(count):
        return [pltpu.VMEM((count, ROWS, D), I16), pltpu.VMEM((count, 1, D), F32)] * 2

    loss, image_dir, text_dir = pl.pallas_call(
        kernel,
        out_shape=(
            jax.ShapeDtypeStruct((8, 128), F32),
            jax.ShapeDtypeStruct((ROWS, D), F32),
            jax.ShapeDtypeStruct((ROWS, D), F32),
        ),
        in_specs=[pl.BlockSpec(memory_space=pl.ANY)] * 5,
        out_specs=(vmem, vmem, vmem),
        scratch_shapes=[
            pltpu.VMEM((ROWS, D), BF16),
            pltpu.VMEM((ROWS, D), BF16),
            pltpu.VMEM((20, 128), jnp.int32),
            pltpu.SMEM((1,), F32),
            pltpu.SMEM((1,), F32),
            pltpu.SemaphoreType.DMA((5,)),
            pltpu.VMEM((SIDE, D), BF16),
            pltpu.VMEM((SIDE, D), BF16),
            pltpu.VMEM((SIDE, SIDE), BF16),
            pltpu.VMEM((SIDE, D), F32),
            pltpu.VMEM((SIDE, D), F32),
            pltpu.VMEM((4, 8, 128), jnp.int32),
            pltpu.VMEM((128, 128), F32),
            pltpu.VMEM((4, 640, 128), F32),
            pltpu.VMEM((SIDE, 128), F32),
            pltpu.VMEM((8, SIDE), F32),
            pltpu.VMEM((8, 128), F32),
            *messages(4),
            *messages(8),
            *messages(4),
            *messages(8),
            *[pltpu.VMEM((8, ROWS, D), I16), pltpu.VMEM((16, 1, D), F32)] * 2,
            pltpu.VMEM((4, 8, 128), F32),
            pltpu.VMEM((4, 8, 128), F32),
            pltpu.VMEM((8, 8, 128), F32),
            pltpu.VMEM((2, 8, 128), F32),
            pltpu.SemaphoreType.DMA((COUNT,)),
            pltpu.SemaphoreType.DMA((COUNT,)),
        ],
        compiler_params=pltpu.CompilerParams(
            collective_id=0, has_side_effects=True, vmem_limit_bytes=60 * 1024 * 1024
        ),
    )(image_emb, text_emb, partner.reshape(20, 128), log_scale, bias)
    loss, grad_image, grad_text = pl.pallas_call(
        finish,
        out_shape=(
            jax.ShapeDtypeStruct((1, 1), F32),
            jax.ShapeDtypeStruct((ROWS, D), F32),
            jax.ShapeDtypeStruct((ROWS, D), F32),
        ),
        in_specs=[vmem] * 5,
        out_specs=(vmem, vmem, vmem),
    )(image_emb, text_emb, loss, image_dir, text_dir)
    return (loss.reshape(1), grad_image, grad_text)


def solution(mesh):
    return jax.shard_map(
        on_device,
        mesh=mesh,
        in_specs=(P(("img", "txt"), None), P(("txt", "img"), None), P("img"), P(), P()),
        out_specs=(P(), P(("img", "txt"), None), P(("txt", "img"), None)),
        check_vma=False,
    )
```

```python
import math

import jax
import jax.numpy as jnp
from jax import lax
from jax.experimental import pallas as pl
from jax.experimental.pallas import tpu as pltpu
from jax.sharding import PartitionSpec as P

MESH = pl.DeviceIdType.MESH
F32, BF16, I16 = jnp.float32, jnp.bfloat16, jnp.int16
ROWS, D = 80, 1152
PAIRS = 20480
SIDE = 16 * ROWS
BUNDLE = 4 * ROWS
OFF4 = (0, 1, 3, 2)
OFF8 = (0, 1, 7, 2, 6, 3, 5, 4)
KEY4 = {off: k for k, off in enumerate(OFF4)}
KEY8 = {off: k for k, off in enumerate(OFF8)}
PIECES = ((0, 48), (48, 32))
FULL = ((0,), (1,))
SUM_PIECES = ((0, 32), (32, 16), (48, 32))
SUM_FULL = ((0, 1), (2,))
CUT = ((0, 48), (48, 32))
FAR_PARTS = (((0, 32), (32, 48)), (None, (0, 80)), ((0, 80), None), CUT)
COUNT = 224


def normalize(emb):
    full = emb.astype(F32)
    inverse = lax.rsqrt(jnp.sum(full * full, axis=1, keepdims=True) + 1e-06)
    return (full * inverse, inverse)


def back_norm(unit, inverse, direction):
    inner = jnp.sum(unit * direction, axis=1, keepdims=True)
    return inverse * (direction - unit * inner)


class Links:
    def __init__(self, send, recv):
        self.send, self.recv = send, recv
        self.sent, self.open = [], []
        self.used = 0

    def tickets(self, count):
        self.used += count
        assert self.used <= COUNT
        return list(range(self.used - count, self.used))

    def start(self, src, dst, ticket, device):
        copy = pltpu.make_async_remote_copy(
            src_ref=src,
            dst_ref=dst,
            send_sem=self.send.at[len(self.sent)],
            recv_sem=self.recv.at[ticket],
            device_id=device,
            device_id_type=MESH,
        )
        copy.start()
        self.sent.append(copy)
        self.open.append(copy)

    def arrived(self, dst, ticket):
        pltpu.make_async_copy(dst, dst, self.recv.at[ticket]).wait()

    def drain(self):
        for copy in self.open:
            copy.wait_send()
        self.open = []


def by_lanes(body):
    def step(n, _):
        for k in range(3):
            body(pl.ds(pl.multiple_of((n * 3 + k) * 128, 128), 128))
        return 0

    lax.fori_loop(0, D // 384, step, 0)


def widen(q, s, rows, lanes):
    return q[rows, lanes].astype(F32) * s[:, lanes]


def narrow(items):
    def body(lanes):
        for value, q, s, rows in items:
            v = value(lanes)
            top = jnp.maximum(jnp.max(jnp.abs(v), axis=0, keepdims=True), 1e-30)
            q[rows, lanes] = jnp.round(v * (32767.0 * pltpu.reciprocal(top, approx=True))).astype(I16)
            s[:, lanes] = top * (1.0 / 32767.0)

    by_lanes(body)


def finish(image_ref, text_ref, loss_part_ref, image_dir_ref, text_dir_ref, loss_ref, grad_image_ref, grad_text_ref):
    loss_ref[...] = loss_part_ref[0:1, 0:1]
    for emb_ref, dir_ref, grad_ref in (
        (image_ref, image_dir_ref, grad_image_ref),
        (text_ref, text_dir_ref, grad_text_ref),
    ):
        unit, inverse = normalize(emb_ref[...])
        grad_ref[...] = back_norm(unit, inverse, dir_ref[...])


def kernel(
    image_hbm, text_hbm, table_hbm, log_scale_hbm, bias_hbm,
    loss_ref, image_dir_ref, text_dir_ref,
    image_ref, text_ref, table_ref, log_scale_ref, bias_ref, load_sems,
    imgs, txts, slopes, pimg, ptxt,
    mates, mate_rows, mate_all, mate_cols, text_ids, loss_acc,
    far_q, far_s, far_qi, far_si,
    near_q, near_s, near_qi, near_si,
    a_q, a_s, a_qi, a_si,
    sib_q, sib_s, sib_qi, sib_si,
    z_q, z_s, z_qi, z_si,
    loss_x, loss_y, loss_z, loss_c,
    send_sems, recv_sems,
):
    img, txt = lax.axis_index("img"), lax.axis_index("txt")
    x, z_hi = img % 4, img // 4
    core, y, z_lo = txt % 2, (txt // 2) % 4, txt // 8
    z = z_hi * 4 + z_lo

    def dev(x, y, z, core):
        return {"img": (z // 4) * 4 + x, "txt": ((z % 4) * 4 + y) * 2 + core}

    def swap(a, b):
        return a + core * (b - a), b + core * (a - b)

    a, b = swap(x, y)

    def plane(a, b):
        px, py = swap(a % 4, b % 4)
        return dev(px, py, z, core)

    def along_z(k):
        return dev(x, y, (z + k) % 8, core)

    to_a = [plane(a + off, b) for off in OFF4]
    to_b = (plane(a, b + 1), plane(a, b + 3))
    to_z = (along_z(1), along_z(7))
    sibling = dev(x, y, z, 1 - core)
    links = Links(send_sems, recv_sems)

    barrier = pltpu.get_barrier_semaphore()
    partners = [dev((x + k) % 4, y, z, core) for k in (1, 2, 3)]
    partners += [dev(x, (y + k) % 4, z, core) for k in (1, 2, 3)]
    partners += [along_z(k) for k in range(1, 8)] + [sibling]
    for device in partners:
        pl.semaphore_signal(barrier, inc=1, device_id=device, device_id_type=MESH)

    loads = [
        pltpu.make_async_copy(src, dst, load_sems.at[k])
        for k, (src, dst) in enumerate((
            (image_hbm, image_ref), (text_hbm, text_ref), (table_hbm, table_ref),
            (log_scale_hbm, log_scale_ref), (bias_hbm, bias_ref),
        ))
    ]
    for load in loads:
        load.start()
    loads[0].wait()
    imgs[0:ROWS, :] = normalize(image_ref[...])[0].astype(BF16)
    loads[1].wait()
    txts[0:ROWS, :] = normalize(text_ref[...])[0].astype(BF16)
    loads[2].wait()
    for k in range(5):
        mates[x, k:k + 1, :] = table_ref[pl.ds(z_lo * 5 + k, 1), :]
    loss_acc[...] = jnp.zeros_like(loss_acc)
    pl.semaphore_wait(barrier, len(partners))

    def img_at(kb, ka):
        return imgs.at[pl.ds((kb * 4 + ka) * ROWS, ROWS), :]

    def txt_at(kz, cc, first=0, count=ROWS):
        return txts.at[pl.ds((kz * 2 + cc) * ROWS + first, count), :]

    ta, ta_far = links.tickets(2), links.tickets(2)
    tb = [links.tickets(4) for _ in range(2)]
    tb_far = [links.tickets(2) for _ in range(4)]
    tz = [[links.tickets(2) for _ in range(4)] for _ in range(2)]
    t_sib = links.tickets(8)
    t_mates = links.tickets(3)

    def b_key(direction):
        return KEY4[3 if direction == 0 else 1]

    def z_key(direction, h):
        return KEY8[-h % 8 if direction == 0 else h]

    def img_part(kb, ka, part):
        return imgs.at[pl.ds((kb * 4 + ka) * ROWS + part[0], part[1]), :]

    def send_a():
        for d in (0, 1):
            links.start(img_at(0, 0), img_at(0, b_key(d)), ta[d], to_a[1 + d])

    def got_a():
        for d in (0, 1):
            links.arrived(img_at(0, b_key(d)), ta[d])
            links.start(img_part(0, b_key(d), CUT[d]), img_part(0, 3, CUT[d]), ta_far[d], to_a[1 + d])

    def got_a_far():
        for d in (0, 1):
            links.arrived(img_part(0, 3, CUT[d]), ta_far[d])

    def send_b(ka):
        for d in (0, 1):
            links.start(img_at(0, ka), img_at(b_key(d), ka), tb[d][ka], to_b[d])

    def got_b(ka):
        for d in (0, 1):
            links.arrived(img_at(b_key(d), ka), tb[d][ka])

    def send_b_far(ka):
        for d in (0, 1):
            part = FAR_PARTS[ka][d]
            if part:
                links.start(img_part(b_key(d), ka, part), img_part(3, ka, part), tb_far[ka][d], to_b[d])

    def got_b_far(ka):
        for d in (0, 1):
            part = FAR_PARTS[ka][d]
            if part:
                links.arrived(img_part(3, ka, part), tb_far[ka][d])

    def send_z(d, h, p):
        first, count = PIECES[p]
        links.start(
            txt_at(z_key(d, h - 1) if h > 1 else 0, 0, first, count),
            txt_at(z_key(d, h), 0, first, count),
            tz[d][h - 1][p],
            to_z[d],
        )

    def got_z(h, p):
        for d in (0, 1):
            if h == 4 and p not in FULL[d]:
                continue
            first, count = PIECES[p]
            links.arrived(txt_at(z_key(d, h), 0, first, count), tz[d][h - 1][p])
            if h < 3 or (h == 3 and p in FULL[d]):
                send_z(d, h + 1, p)


    def send_sib(kz):
        links.start(txt_at(kz, 0), txt_at(kz, 1), t_sib[kz], sibling)

    def got_sib(kz):
        links.arrived(txt_at(kz, 1), t_sib[kz])

    send_a()
    for p in (0, 1):
        for d in (0, 1):
            send_z(d, 1, p)

    column = lax.broadcasted_iota(jnp.int32, (8, SIDE), 1)
    ids = column
    for kz in range(8):
        for cc in (0, 1):
            slot, pz = kz * 2 + cc, (z + OFF8[kz]) % 8
            c = core if cc == 0 else 1 - core
            start = ((((pz % 4) * 4 + y) * 2 + c) * 8 + (pz // 4) * 4 + x) * ROWS
            ids = jnp.where(column >= slot * ROWS, column - slot * ROWS + start, ids)
    text_ids[...] = ids.astype(F32)

    for copy in links.open[0:2]:
        copy.wait_send()
    links.open = links.open[2:]
    send_b(0)
    send_sib(0)
    for k in (1, 2, 3):
        links.start(mates.at[x], mates.at[x], t_mates[k - 1], partners[k - 1])
    got_z(1, 0)
    got_a()
    send_b(1)
    send_b(2)
    for k in (1, 2, 3):
        links.arrived(mates.at[(x + 4 - k) % 4], t_mates[k - 1])
    mate_rows[...] = jnp.zeros_like(mate_rows)
    for px in range(4):
        mate_rows[px * 8:px * 8 + 5, :] = mates[px, 0:5, :].astype(F32)
    turned = mate_rows[...].T
    for px in range(4):
        for k in range(5):
            mate_all[px, k * 128:(k + 1) * 128, :] = jnp.broadcast_to(
                turned[:, px * 8 + k:px * 8 + k + 1], (128, 128)
            )
    for kb in range(4):
        for ka in range(4):
            px, py = swap((a + OFF4[ka]) % 4, (b + OFF4[kb]) % 4)
            start = pl.multiple_of((2 * py + core) * ROWS, 16)
            mate_cols[(kb * 4 + ka) * ROWS:(kb * 4 + ka + 1) * ROWS, :] = mate_all[px, pl.ds(start, ROWS), :]

    got_z(1, 1)
    send_sib(1)
    send_sib(2)
    got_a_far()
    send_b(3)
    got_z(2, 0)

    loads[3].wait()
    loads[4].wait()
    scale = jnp.exp(jnp.full((1, 1), log_scale_ref[0], F32))
    to_log2 = scale * math.log2(math.e)
    shift = jnp.full((1, 1), bias_ref[0] * math.log2(math.e), F32)

    def tile(kb, top, height, first, count):
        rows = pl.ds(kb * BUNDLE + top if isinstance(kb, int) else pl.multiple_of(kb * BUNDLE + top, 16), height)
        cols = pl.ds(first, count)
        cosine = lax.dot_general(
            imgs[rows, :], txts[cols, :], (((1,), (1,)), ((), ())), preferred_element_type=F32
        )
        logits = cosine * to_log2 + shift
        e = jnp.exp2(logits)
        u = 1.0 + e
        r = pltpu.reciprocal(u, approx=True)
        mate = mate_cols[rows, :]
        positive = jnp.concatenate([mate] * (count // 128), axis=1) == text_ids[0:1, cols]
        slopes[rows, cols] = jnp.where(positive, -r, e * r).astype(BF16)
        paired = jnp.where(positive, logits, 0.0)
        grown = [e[k:k + ROWS] for k in range(0, height, ROWS)]
        while len(grown) > 1:
            first_e, second_e, *others = grown
            grown = [*others, first_e + second_e + first_e * second_e]
        over = 1.0 + grown[0]
        lost = jnp.log(over) + (grown[0] - (over - 1.0)) * pltpu.reciprocal(over, approx=True)
        total = lost.reshape(10, 8, count).sum(0)
        total -= paired.reshape(height // 8, 8, count).sum(0) * math.log(2.0)
        folded = total[:, 0:128]
        for k in range(128, count, 128):
            folded = folded + total[:, k:k + 128]
        loss_acc[...] += folded

    def text_part(first, count, low=0, high=SIDE):
        rows, depth = pl.ds(first, count), pl.ds(low, high - low)
        part = lax.dot_general(
            slopes[depth, rows], imgs[depth, :], (((0,), (0,)), ((), ())), preferred_element_type=F32
        )
        if low:
            ptxt[rows, :] += part
        else:
            ptxt[rows, :] = part

    def tiles(low, high, top, height, first, count):
        def step(kb, _):
            tile(kb, top, height, first, count)
            return 0

        lax.fori_loop(low, high, step, 0)

    got_z(2, 1)
    send_sib(3)
    send_sib(4)
    got_b(1)
    send_b_far(1)
    got_b(2)
    send_b_far(2)
    got_b(0)
    send_b_far(0)
    for kz in (0, 1, 2, 3, 4):
        got_sib(kz)
    tile(0, 0, BUNDLE, 0, 768)
    got_z(3, 0)
    got_z(3, 1)
    send_sib(5)
    send_sib(6)
    got_b(3)
    send_b_far(3)
    tiles(1, 3, 0, BUNDLE, 0, 768)
    text_part(0, 384, 0, 960)
    for p in (0, 1):
        got_z(4, p)
    send_sib(7)
    text_part(384, 384, 0, 960)
    got_sib(5)
    got_sib(6)
    got_sib(7)
    tiles(0, 3, 0, BUNDLE, 768, 512)

    lx, ly, lz, lc = links.tickets(3), links.tickets(3), links.tickets(7), links.tickets(1)

    def share(buffer, me, size, tickets, devices):
        for k in range(1, size):
            links.start(buffer.at[me], buffer.at[me], tickets[k - 1], devices[k - 1])

    def gathered(buffer, me, size, tickets):
        for k in range(1, size):
            links.arrived(buffer.at[(me + size - k) % size], tickets[k - 1])
        total = buffer[0]
        for k in range(1, size):
            total = total + buffer[k]
        return total

    def image_part(kb):
        rows = pl.ds(kb * BUNDLE, BUNDLE)
        pimg[rows, :] = jnp.dot(slopes[rows, :], txts[...], preferred_element_type=F32)

    whole = pl.ds(0, ROWS)

    def send_pair(q, s, q_in, s_in, tickets, device):
        links.start(q, q_in, tickets[0], device)
        links.start(s, s_in, tickets[1], device)

    def got_pair(q_in, s_in, tickets):
        links.arrived(q_in, tickets[0])
        links.arrived(s_in, tickets[1])

    def img_rows(kb, ka):
        return pl.ds((kb * 4 + ka) * ROWS, ROWS)

    FAR = ((3, 2), (1, 0))
    u_far = {ka: links.tickets(2) for ka in range(4)}
    u_near = [{ka: links.tickets(2) for ka in range(4)} for _ in range(2)]
    u_a = {ka: links.tickets(2) for ka in (1, 2, 3)}
    u_sib = [links.tickets(2) for _ in range(8)]
    u_z = [[[links.tickets(2) for _ in range(3)] for _ in range(4)] for _ in range(2)]

    def send_far(n):
        items = []
        for d in (0, 1):
            rows = img_rows(3, FAR[d][n])
            items.append((lambda lanes, rows=rows: pimg[rows, lanes], far_q.at[FAR[d][n]], far_s.at[FAR[d][n]], whole))
        narrow(items)
        for d in (0, 1):
            ka = FAR[d][n]
            send_pair(far_q.at[ka], far_s.at[ka], far_qi.at[ka], far_si.at[ka], u_far[ka], to_b[d])

    sent_near = []

    def send_near(pairs):
        items = []
        for d, ka in pairs:
            rows = img_rows(KEY4[1 if d == 0 else 3], ka)
            if ka in FAR[d]:
                got_pair(far_qi.at[ka], far_si.at[ka], u_far[ka])

            def value(lanes, d=d, ka=ka, rows=rows):
                v = pimg[rows, lanes]
                return v + widen(far_qi.at[ka], far_si.at[ka], whole, lanes) if ka in FAR[d] else v

            items.append((value, near_q.at[d * 4 + ka], near_s.at[d * 4 + ka], whole))
        narrow(items)
        for d in (0, 1):
            kas = [ka for e, ka in pairs if e == d]
            if kas:
                n = pl.ds(d * 4 + min(kas), len(kas))
                send_pair(near_q.at[n], near_s.at[n], near_qi.at[n], near_si.at[n], u_near[d][min(kas)], to_b[d])
                sent_near.append((d, tuple(kas)))

    def fold(ka):
        for d, kas in list(sent_near):
            if ka in kas:
                n = pl.ds(d * 4 + min(kas), len(kas))
                got_pair(near_qi.at[n], near_si.at[n], u_near[d][min(kas)])
                sent_near.remove((d, kas))

        def value(lanes):
            v = pimg[img_rows(0, ka), lanes]
            return v + widen(near_qi.at[ka], near_si.at[ka], whole, lanes) + widen(
                near_qi.at[4 + ka], near_si.at[4 + ka], whole, lanes
            )

        if ka:
            narrow([(value, a_q.at[ka], a_s.at[ka], whole)])
            send_pair(a_q.at[ka], a_s.at[ka], a_qi.at[ka], a_si.at[ka], u_a[ka], to_a[ka])
        else:
            def body(lanes):
                pimg[0:ROWS, lanes] = value(lanes)

            by_lanes(body)

    def swap_text(keys):
        items = []
        for kz in keys:
            rows = pl.ds((kz * 2 + 1) * ROWS, ROWS)
            items.append((lambda lanes, rows=rows: ptxt[rows, lanes], sib_q.at[kz], sib_s.at[kz], whole))
        narrow(items)
        for kz in keys:
            send_pair(sib_q.at[kz], sib_s.at[kz], sib_qi.at[kz], sib_si.at[kz], u_sib[kz], sibling)

    def got_swap(kz):
        got_pair(sib_qi.at[kz], sib_si.at[kz], u_sib[kz])

    def z_piece(buffer, d, r, p):
        return buffer.at[d * 4 + r - 1, pl.ds(*SUM_PIECES[p]), :]

    def z_step(d, r, p):
        return (d * 4 + r - 1) * 3 + p

    def got_zsum(d, r, p):
        got_pair(z_piece(z_qi, d, r, p), z_si.at[z_step(d, r, p)], u_z[d][r - 1][p])

    LONG, MIDDLE, SHORT = ((0, 0), (2, 1)), ((1, 0),), ((2, 0), (0, 1), (1, 1))

    def send_zsum(r, chains):
        items = []
        for p, d in chains:
            first, count = SUM_PIECES[p]
            kz = KEY8[r % 8 if d == 0 else -r % 8]
            added = r < 3 or (r == 3 and p in SUM_FULL[d])
            if added:
                got_zsum(d, r + 1, p)
            here = pl.ds(first, count)

            def value(lanes, d=d, p=p, first=first, count=count, kz=kz, added=added, here=here):
                v = ptxt[pl.ds(kz * 2 * ROWS + first, count), lanes] + widen(sib_qi.at[kz], sib_si.at[kz], here, lanes)
                if added:
                    v = v + widen(z_qi.at[d * 4 + r], z_si.at[z_step(d, r + 1, p)], here, lanes)
                return v

            items.append((value, z_q.at[d * 4 + r - 1], z_s.at[z_step(d, r, p)], here))
        narrow(items)
        for p, d in chains:
            n = z_step(d, r, p)
            send_pair(
                z_piece(z_q, d, r, p), z_s.at[n], z_piece(z_qi, d, r, p), z_si.at[n], u_z[d][r - 1][p], to_z[d]
            )

    for ka in (2, 1, 0, 3):
        got_b_far(ka)
    tile(3, 0, BUNDLE, 0, SIDE)
    text_part(768, 512)
    swap_text((7, 5, 6))
    image_part(3)
    send_far(0)
    send_far(1)
    got_swap(7)
    send_zsum(4, LONG)
    send_zsum(4, MIDDLE)
    got_swap(5)
    got_swap(6)
    send_zsum(3, SHORT)
    part = jnp.sum(jnp.sum(loss_acc[...], axis=0, keepdims=True), axis=1, keepdims=True)
    loss_x[x] = jnp.broadcast_to(part, (8, 128))
    share(loss_x, x, 4, lx, partners[0:3])
    image_part(1)
    send_near(((0, 1), (0, 0)))
    image_part(2)
    send_near(((1, 3), (1, 2)))
    text_part(0, 768, 960, SIDE)
    swap_text((3, 4, 2, 1, 0))
    send_zsum(3, LONG)
    send_zsum(3, MIDDLE)
    send_near(((0, 3), (1, 1)))
    image_part(0)
    loss_y[y] = gathered(loss_x, x, 4, lx)
    share(loss_y, y, 4, ly, partners[3:6])
    got_swap(3)
    got_swap(4)
    send_zsum(2, SHORT)
    send_near(((0, 2), (1, 0)))
    fold(3)
    send_zsum(2, LONG)
    send_zsum(2, MIDDLE)
    loss_z[z] = gathered(loss_y, y, 4, ly)
    share(loss_z, z, 8, lz, partners[6:13])
    got_swap(1)
    got_swap(2)
    send_zsum(1, SHORT)
    fold(1)
    fold(2)
    send_zsum(1, LONG)
    send_zsum(1, MIDDLE)
    fold(0)
    loss_c[core] = gathered(loss_z, z, 8, lz)
    share(loss_c, core, 2, lc, [sibling])
    got_swap(0)

    for ka in (1, 2, 3):
        got_pair(a_qi.at[ka], a_si.at[ka], u_a[ka])

    def image_sum(lanes):
        v = pimg[0:ROWS, lanes]
        for ka in (1, 2, 3):
            v = v + widen(a_qi.at[ka], a_si.at[ka], whole, lanes)
        image_dir_ref[:, lanes] = v * scale

    by_lanes(image_sum)

    for p, d in (*SHORT, *LONG, *MIDDLE):
        got_zsum(d, 1, p)

    def text_sum(lanes):
        for p, (first, count) in enumerate(SUM_PIECES):
            here = pl.ds(first, count)
            v = ptxt[here, lanes] + widen(sib_qi.at[0], sib_si.at[0], here, lanes)
            for d in (0, 1):
                v = v + widen(z_qi.at[d * 4], z_si.at[z_step(d, 1, p)], here, lanes)
            text_dir_ref[here, lanes] = v * scale

    by_lanes(text_sum)
    loss_ref[...] = gathered(loss_c, core, 2, lc) * (1.0 / PAIRS)
    links.drain()


def on_device(image_emb, text_emb, partner, log_scale, bias):
    vmem = pl.BlockSpec(memory_space=pltpu.VMEM)

    def messages(count):
        return [pltpu.VMEM((count, ROWS, D), I16), pltpu.VMEM((count, 1, D), F32)] * 2

    loss, image_dir, text_dir = pl.pallas_call(
        kernel,
        out_shape=(
            jax.ShapeDtypeStruct((8, 128), F32),
            jax.ShapeDtypeStruct((ROWS, D), F32),
            jax.ShapeDtypeStruct((ROWS, D), F32),
        ),
        in_specs=[pl.BlockSpec(memory_space=pl.ANY)] * 5,
        out_specs=(vmem, vmem, vmem),
        scratch_shapes=[
            pltpu.VMEM((ROWS, D), BF16),
            pltpu.VMEM((ROWS, D), BF16),
            pltpu.VMEM((20, 128), jnp.int32),
            pltpu.SMEM((1,), F32),
            pltpu.SMEM((1,), F32),
            pltpu.SemaphoreType.DMA((5,)),
            pltpu.VMEM((SIDE, D), BF16),
            pltpu.VMEM((SIDE, D), BF16),
            pltpu.VMEM((SIDE, SIDE), BF16),
            pltpu.VMEM((SIDE, D), F32),
            pltpu.VMEM((SIDE, D), F32),
            pltpu.VMEM((4, 8, 128), jnp.int32),
            pltpu.VMEM((128, 128), F32),
            pltpu.VMEM((4, 640, 128), F32),
            pltpu.VMEM((SIDE, 128), F32),
            pltpu.VMEM((8, SIDE), F32),
            pltpu.VMEM((8, 128), F32),
            *messages(4),
            *messages(8),
            *messages(4),
            *messages(8),
            *[pltpu.VMEM((8, ROWS, D), I16), pltpu.VMEM((24, 1, D), F32)] * 2,
            pltpu.VMEM((4, 8, 128), F32),
            pltpu.VMEM((4, 8, 128), F32),
            pltpu.VMEM((8, 8, 128), F32),
            pltpu.VMEM((2, 8, 128), F32),
            pltpu.SemaphoreType.DMA((COUNT,)),
            pltpu.SemaphoreType.DMA((COUNT,)),
        ],
        compiler_params=pltpu.CompilerParams(
            collective_id=0, has_side_effects=True, vmem_limit_bytes=60 * 1024 * 1024
        ),
    )(image_emb, text_emb, partner.reshape(20, 128), log_scale, bias)
    loss, grad_image, grad_text = pl.pallas_call(
        finish,
        out_shape=(
            jax.ShapeDtypeStruct((1, 1), F32),
            jax.ShapeDtypeStruct((ROWS, D), F32),
            jax.ShapeDtypeStruct((ROWS, D), F32),
        ),
        in_specs=[vmem] * 5,
        out_specs=(vmem, vmem, vmem),
    )(image_emb, text_emb, loss, image_dir, text_dir)
    return (loss.reshape(1), grad_image, grad_text)


def solution(mesh):
    return jax.shard_map(
        on_device,
        mesh=mesh,
        in_specs=(P(("img", "txt"), None), P(("txt", "img"), None), P("img"), P(), P()),
        out_specs=(P(), P(("img", "txt"), None), P(("txt", "img"), None)),
        check_vma=False,
    )
```
